32 devices in a mesh: row: 2 (over y), col: 4 (over z), depth: 4 (over x, core).
Axes of the slice: x: 2, y: 2, z: 4, core: 2. Of those that a mesh axis runs over, the one named last changes fastest.
Arguments:
- integrals: float32 [4096, 4096], P(('row', 'col'), 'depth'), may hold values from -0.09375 to 0.09375
- amplitudes: float32 [4096, 64, 64], P('depth', 'col', 'row'), may hold values from -6 to 6
Outputs:
- relaid: float32 [64, 64, 4096], P(('col', 'depth'), 'row')
The draws below stay inside these ranges and needn't reach their ends.
All inputs are finite; a program needn't handle non-finite values.
Results may differ from the reference program's by a relative error of at most 0.00007.
Values sent between devices are 32-bit elements; how exact they have to be, the bound alone decides.
A program may use at most 64 MiB of HBM per device.

```python
import jax
import jax.numpy as jnp
from jax import lax

O = 64
AB = 4096
KC = 4096
N_ROW = 2


def levels(stream_key, extent, split, low, largest):
    factor_of, own = 1.0, jax.random.fold_in(stream_key, 6)
    for position, parts in split:
        draws = jnp.exp(jax.random.uniform(jax.random.fold_in(own, position), (parts,), jnp.float32, low / len(split), largest / len(split)))
        factor_of = factor_of * jnp.repeat(draws, extent[position] // parts).reshape([-1 if axis == position else 1 for axis in range(len(extent))])
    return factor_of


def gaussian(stream_key, dims, scale, reach, split=(), dtype=jnp.bfloat16):
    drawn = jax.random.normal(stream_key, dims, jnp.float32) * scale
    if len(split) > 0:
        drawn = levels(stream_key, dims, split, -0.22, 0.18) * drawn
    return jnp.clip(drawn, min=-reach, max=reach).astype(dtype)


def setup_inputs(seed: int = 0) -> dict:
    arg_keys = jax.random.split(jax.random.key(seed), 3)
    integrals = gaussian(arg_keys[0], (AB, KC), KC ** -0.5, 0.09375, ((0, 8), (1, 4)), jnp.float32)
    amplitudes = gaussian(arg_keys[1], (KC, O, O), 1.0, 6.0, ((0, 4), (1, 4), (2, 2)), jnp.float32)
    return dict(integrals=integrals, amplitudes=amplitudes)


def reference(integrals, amplitudes):
    shaped = amplitudes.reshape(KC, O, O // N_ROW, N_ROW)
    relaid = jnp.einsum("ak,kitr->irta", integrals, shaped, precision=lax.Precision.HIGHEST, preferred_element_type=jnp.float32)
    return relaid.reshape(O, O, AB)
```

```python
import functools

import jax
import jax.numpy as jnp
import numpy as np
from jax import lax
from jax.experimental import pallas as pl
from jax.experimental.pallas import tpu as pltpu
from jax.sharding import PartitionSpec as P

MESH = pl.DeviceIdType.MESH
CHUNK = 256
LANES = 2


def halves(x):
    hi = x.astype(jnp.bfloat16)
    lo = (x - hi.astype(jnp.float32)).astype(jnp.bfloat16)
    return hi, lo


def kernel(sizes, gathered, w_ref, t_ref, order_ref, out_ref, wg, tg, th, tl, part, recv1, recv2, fin,
           own_sem, w_send, w_recv, t_send, t_recv, s1_send, s1_recv, s2_send, s2_recv, r_send, r_recv):
    n_row, n_col, n_depth = sizes
    n_lo = LANES
    n_hi = n_depth // n_lo
    ab_rows = w_ref.shape[0]
    n_ch = ab_rows // CHUNK
    steps = n_col * n_ch
    rows_all = th.shape[0]
    rows_lo = rows_all // n_lo
    rows_d = rows_lo // n_hi
    rows_r = rows_d // n_row
    row, col, depth = lax.axis_index("row"), lax.axis_index("col"), lax.axis_index("depth")
    hi, lo = depth // n_lo, depth % n_lo

    def row_peer(o):
        return (row + o) % n_row

    def hi_peer(o):
        return (hi + o) % n_hi

    mate = hi * n_lo + (1 - lo)

    barrier = pltpu.get_barrier_semaphore()
    for o in range(1, n_row):
        pl.semaphore_signal(barrier, inc=1, device_id={"row": row_peer(o)}, device_id_type=MESH)
    pl.semaphore_signal(barrier, inc=1, device_id={"depth": mate}, device_id_type=MESH)
    for o in range(1, n_hi):
        pl.semaphore_signal(barrier, inc=1, device_id={"depth": hi_peer(o) * n_lo + lo}, device_id_type=MESH)

    @pl.when(col > 0)
    def _():
        pl.semaphore_signal(barrier, inc=1, device_id={"col": col - 1}, device_id_type=MESH)

    @pl.when(col < n_col - 1)
    def _():
        pl.semaphore_signal(barrier, inc=1, device_id={"col": col + 1}, device_id_type=MESH)

    fixed = (n_row - 1) + 1 + (n_hi - 1)
    ends = jnp.where(col > 0, 1, 0) + jnp.where(col < n_col - 1, 1, 0)
    pl.semaphore_wait(barrier, fixed + ends)

    def w_copy(src, b, h, side):
        rows = pl.ds(pl.multiple_of(h * CHUNK, CHUNK), CHUNK)
        to = jnp.clip(col + (1 if side else -1), 0, n_col - 1)
        return pltpu.make_async_remote_copy(
            src_ref=w_ref.at[rows] if src is None else wg.at[b, rows],
            dst_ref=wg.at[b, rows],
            send_sem=w_send.at[side, b, h],
            recv_sem=w_recv.at[b, h],
            device_id={"col": to},
            device_id_type=MESH,
        )

    def send_own(h, c):
        @pl.when(col > 0)
        def _():
            w_copy(None, col, h, 0).start()

        @pl.when(col < n_col - 1)
        def _():
            w_copy(None, col, h, 1).start()

        return c

    lax.fori_loop(0, n_ch, send_own, 0)

    def t_copy(o):
        return pltpu.make_async_remote_copy(
            src_ref=t_ref,
            dst_ref=tg.at[row],
            send_sem=t_send.at[o - 1],
            recv_sem=t_recv.at[o - 1],
            device_id={"row": row_peer(o)},
            device_id_type=MESH,
        )

    if not gathered:
        for o in range(1, n_row):
            t_copy(o).start()
        t_own = pltpu.make_async_copy(t_ref, tg.at[row], own_sem.at[1])
    else:
        t_own = pltpu.make_async_copy(t_ref, tg, own_sem.at[1])
    t_own.start()
    w_own = pltpu.make_async_copy(w_ref, wg.at[col], own_sem.at[0])
    w_own.start()

    def place(q):
        i_count, j_local, kc = t_ref.shape
        i_out = i_count // n_depth
        per_r = j_local // n_row
        order = order_ref[...]

        def body(d, c):
            x = tg[q, pl.ds(d * i_out, i_out)].reshape(i_out * j_local, kc)
            base = (d % n_lo) * rows_lo + (d // n_lo) * rows_d
            for x_part, into in zip(halves(x), (th, tl)):
                y = jnp.dot(order, x_part, preferred_element_type=jnp.float32).astype(jnp.bfloat16)
                for piece in range(n_row * i_out):
                    at = base + piece * (per_r * n_row) + q * per_r
                    into[pl.ds(pl.multiple_of(at, per_r), per_r), :] = y[piece * per_r : (piece + 1) * per_r]
            return c

        lax.fori_loop(0, n_depth, body, 0)

    t_own.wait()
    if not gathered:
        place(row)
    else:
        def body(m, c):
            at = pl.ds(pl.multiple_of(m * 64, 64), 64)
            th[at, :], tl[at, :] = halves(tg[at, :])
            return c

        lax.fori_loop(0, rows_all // 64, body, 0)

    def forward(b, h):
        w_copy(wg, b, h, 0).wait_recv()

        @pl.when((b < col) & (col < n_col - 1))
        def _():
            w_copy(wg, b, h, 1).start()

        @pl.when((b > col) & (col > 0))
        def _():
            w_copy(wg, b, h, 0).start()

    def first(h, c):
        @pl.when(col > 0)
        def _():
            forward(col - 1, h)

        @pl.when(col < n_col - 1)
        def _():
            forward(col + 1, h)

        return c

    lax.fori_loop(0, n_ch, first, 0)

    if not gathered:
        for o in range(1, n_row):
            t_copy(o).wait_recv()
            place((row + n_row - o) % n_row)
    w_own.wait()

    near = jnp.minimum(col, n_col - 1 - col)

    def block_at(k):
        p, h = k // n_ch, k % n_ch
        both = p <= 2 * near
        s = jnp.where(both, (p + 1) // 2, p - near)
        left = jnp.where(both, p % 2 == 1, col > near)
        b = jnp.where(p == 0, col, jnp.where(left, col - s, col + s))
        return b, h, s

    def s1_copy(k):
        return pltpu.make_async_remote_copy(
            src_ref=part.at[k, pl.ds(pl.multiple_of((1 - lo) * rows_lo, rows_lo), rows_lo)],
            dst_ref=recv1.at[k],
            send_sem=s1_send.at[k],
            recv_sem=s1_recv.at[k],
            device_id={"depth": mate},
            device_id_type=MESH,
        )

    def s2_copy(k, o):
        return pltpu.make_async_remote_copy(
            src_ref=part.at[k, pl.ds(pl.multiple_of(lo * rows_lo + hi_peer(o) * rows_d, rows_d), rows_d)],
            dst_ref=recv2.at[k, o - 1],
            send_sem=s2_send.at[k, o - 1],
            recv_sem=s2_recv.at[k, o - 1],
            device_id={"depth": hi_peer(o) * n_lo + lo},
            device_id_type=MESH,
        )

    def out_cols(k):
        b, h, _ = block_at(k)
        return pl.ds(pl.multiple_of((row * n_col + b) * ab_rows + h * CHUNK, CHUNK), CHUNK)

    def r_copy(k, o):
        return pltpu.make_async_remote_copy(
            src_ref=fin.at[k, pl.ds(pl.multiple_of(row_peer(o) * rows_r, rows_r), rows_r)],
            dst_ref=out_ref.at[:, out_cols(k)],
            send_sem=r_send.at[k, o - 1],
            recv_sem=r_recv.at[k, o - 1],
            device_id={"row": row_peer(o)},
            device_id_type=MESH,
        )

    def dot(a, b):
        return lax.dot_general(a, b, (((1,), (1,)), ((), ())), preferred_element_type=jnp.float32)

    def step(k, c):
        @pl.when(k < steps)
        def _():
            b, h, s = block_at(k)

            @pl.when(s >= 2)
            def _():
                forward(b, h)

            wh, wl = halves(wg[b, pl.ds(pl.multiple_of(h * CHUNK, CHUNK), CHUNK), :])
            tile = rows_all // 2
            for m in range(2):
                at = pl.ds(m * tile, tile)
                a = th[at, :]
                part[k, at, :] = dot(a, wh) + dot(a, wl) + dot(tl[at, :], wh)
            s1_copy(k).start()

        @pl.when((k >= 1) & (k < steps + 1))
        def _():
            j = k - 1
            s1_copy(j).wait_recv()
            at = pl.ds(pl.multiple_of(lo * rows_lo, rows_lo), rows_lo)
            part[j, at, :] = part[j, at, :] + recv1[j]
            for o in range(1, n_hi):
                s2_copy(j, o).start()

        @pl.when(k >= 2)
        def _():
            j = k - 2
            total = part[j, pl.ds(pl.multiple_of(lo * rows_lo + hi * rows_d, rows_d), rows_d), :]
            for o in range(1, n_hi):
                s2_copy(j, o).wait_recv()
                total = total + recv2[j, o - 1]
            fin[j] = total
            for o in range(1, n_row):
                r_copy(j, o).start()
            out_ref[:, out_cols(j)] = fin[j, pl.ds(pl.multiple_of(row * rows_r, rows_r), rows_r), :]

        return c

    lax.fori_loop(0, steps + 2, step, 0)

    def drain(k, c):
        s1_copy(k).wait_send()
        for o in range(1, n_hi):
            s2_copy(k, o).wait_send()
        for o in range(1, n_row):
            r_copy(k, o).wait_send()
            r_copy(k, o).wait_recv()
        b, h = k // n_ch, k % n_ch

        @pl.when((b <= col) & (col < n_col - 1))
        def _():
            w_copy(wg, b, h, 1).wait_send()

        @pl.when((b >= col) & (col > 0))
        def _():
            w_copy(wg, b, h, 0).wait_send()

        return c

    lax.fori_loop(0, steps, drain, 0)
    if not gathered:
        for o in range(1, n_row):
            t_copy(o).wait_send()


def shards(sizes, integrals, amplitudes):
    n_row, n_col, n_depth = sizes
    n_lo = LANES
    n_hi = n_depth // n_lo
    kc, i_count, j_local = amplitudes.shape
    j_count = j_local * n_row
    ab_rows = integrals.shape[0]
    steps = n_col * (ab_rows // CHUNK)
    rows_all = i_count * j_count
    rows_lo = rows_all // n_lo
    rows_d = rows_lo // n_hi
    rows_r = rows_d // n_row
    i_out = i_count // n_depth
    gathered = j_local % (16 * n_row) != 0
    side = i_out * j_local
    tiny = j_local if gathered else n_row
    source = np.arange(side).reshape(i_out, j_local // tiny, tiny).transpose(2, 0, 1).reshape(-1)
    order = jnp.asarray(np.eye(side)[source], jnp.bfloat16)
    t = jnp.transpose(amplitudes, (1, 2, 0))
    if gathered:
        t = lax.all_gather(t, "row", axis=1, tiled=True)
        t = t.reshape(n_hi, n_lo, i_out, j_count // n_row, n_row, kc)
        t = jnp.transpose(t, (1, 0, 4, 2, 3, 5)).reshape(rows_all, kc)
        tg = pltpu.VMEM(t.shape, jnp.float32)
    else:
        tg = pltpu.VMEM((n_row,) + t.shape, jnp.float32)
    dma = pltpu.SemaphoreType.DMA
    out = pl.pallas_call(
        functools.partial(kernel, sizes, gathered),
        out_shape=jax.ShapeDtypeStruct((rows_r, n_row * n_col * ab_rows), jnp.float32),
        in_specs=[pl.BlockSpec(memory_space=pl.ANY)] * 2 + [pl.BlockSpec(memory_space=pltpu.VMEM)],
        out_specs=pl.BlockSpec(memory_space=pltpu.VMEM),
        scratch_shapes=[
            pltpu.VMEM((n_col, ab_rows, kc), jnp.float32),
            tg,
            pltpu.VMEM((rows_all, kc), jnp.bfloat16),
            pltpu.VMEM((rows_all, kc), jnp.bfloat16),
            pltpu.VMEM((steps, rows_all, CHUNK), jnp.float32),
            pltpu.VMEM((steps, rows_lo, CHUNK), jnp.float32),
            pltpu.VMEM((steps, max(n_hi - 1, 1), rows_d, CHUNK), jnp.float32),
            pltpu.VMEM((steps, rows_d, CHUNK), jnp.float32),
            dma((2,)),
            dma((2, n_col, ab_rows // CHUNK)),
            dma((n_col, ab_rows // CHUNK)),
            dma((max(n_row - 1, 1),)),
            dma((max(n_row - 1, 1),)),
            dma((steps,)),
            dma((steps,)),
            dma((steps, max(n_hi - 1, 1))),
            dma((steps, max(n_hi - 1, 1))),
            dma((steps, max(n_row - 1, 1))),
            dma((steps, max(n_row - 1, 1))),
        ],
        compiler_params=pltpu.CompilerParams(
            collective_id=0, has_side_effects=True, vmem_limit_bytes=60 * 2**20
        ),
        cost_estimate=pl.CostEstimate(
            flops=6 * rows_all * kc * ab_rows * n_col, bytes_accessed=6 * 2**20, transcendentals=0
        ),
    )(integrals, t, order)
    return out.reshape(i_out, j_count // n_row, n_row * n_col * ab_rows)


def solution(mesh):
    sizes = (mesh.shape["row"], mesh.shape["col"], mesh.shape["depth"])
    placed = (P(("row", "col"), "depth"), P("depth", "col", "row"))
    return jax.shard_map(
        functools.partial(shards, sizes),
        mesh=mesh,
        in_specs=placed,
        out_specs=P(("col", "depth"), "row", None),
        check_vma=False,
    )
```

```python
import functools

import jax
import jax.numpy as jnp
import numpy as np
from jax import lax
from jax.experimental import pallas as pl
from jax.experimental.pallas import tpu as pltpu
from jax.sharding import PartitionSpec as P

MESH = pl.DeviceIdType.MESH
CHUNK = 256
LANES = 2


def halves(x):
    hi = x.astype(jnp.bfloat16)
    lo = (x - hi.astype(jnp.float32)).astype(jnp.bfloat16)
    return hi, lo


def kernel(sizes, gathered, w_ref, t_ref, order_ref, out_ref, wg, tg, tg2, th, tl, part, recv1, recv2, fin,
           own_sem, w_send, w_recv, t_send, t_recv, s1_send, s1_recv, s2_send, s2_recv, r_send, r_recv,
           e_send, e_recv, x_send, x_recv, d_send, d_recv):
    n_row, n_col, n_depth = sizes
    n_lo = LANES
    n_hi = n_depth // n_lo
    ab_rows = w_ref.shape[0]
    n_ch = ab_rows // CHUNK
    steps = n_col * n_ch
    rows_all = th.shape[1]
    rows_lo = rows_all // n_lo
    rows_d = rows_lo // n_hi
    rows_r = rows_d // n_row
    row, col, depth = lax.axis_index("row"), lax.axis_index("col"), lax.axis_index("depth")
    hi, lo = depth // n_lo, depth % n_lo

    def row_peer(o):
        return (row + o) % n_row

    def hi_peer(o):
        return (hi + o) % n_hi

    mate = hi * n_lo + (1 - lo)
    at_end = (col == 0) | (col == n_col - 1)
    helps = (col == 1) | (col == n_col - 2)
    far = jnp.where(col < n_col // 2, n_col - 1, 0)
    end_col = jnp.where(col < n_col // 2, 0, n_col - 1)
    help_col = jnp.where(col < n_col // 2, 1, n_col - 2)
    normal = jnp.where(at_end, steps - n_ch, steps)
    total_steps = jnp.where(helps, steps + n_ch, normal)

    barrier = pltpu.get_barrier_semaphore()
    for o in range(1, n_row):
        pl.semaphore_signal(barrier, inc=1, device_id={"row": row_peer(o)}, device_id_type=MESH)
    pl.semaphore_signal(barrier, inc=1, device_id={"depth": mate}, device_id_type=MESH)
    for o in range(1, n_hi):
        pl.semaphore_signal(barrier, inc=1, device_id={"depth": hi_peer(o) * n_lo + lo}, device_id_type=MESH)

    @pl.when(col > 0)
    def _():
        pl.semaphore_signal(barrier, inc=1, device_id={"col": col - 1}, device_id_type=MESH)

    @pl.when(col < n_col - 1)
    def _():
        pl.semaphore_signal(barrier, inc=1, device_id={"col": col + 1}, device_id_type=MESH)

    for o in range(1, n_row):

        @pl.when(at_end)
        def _():
            pl.semaphore_signal(
                barrier, inc=1, device_id={"row": row_peer(o), "col": help_col}, device_id_type=MESH
            )

        @pl.when(helps)
        def _():
            pl.semaphore_signal(
                barrier, inc=1, device_id={"row": row_peer(o), "col": end_col}, device_id_type=MESH
            )

    fixed = (n_row - 1) + 1 + (n_hi - 1)
    ends = jnp.where(col > 0, 1, 0) + jnp.where(col < n_col - 1, 1, 0)
    diagonal = jnp.where(at_end | helps, n_row - 1, 0)
    pl.semaphore_wait(barrier, fixed + ends + diagonal)

    def w_copy(src, b, h, side):
        rows = pl.ds(pl.multiple_of(h * CHUNK, CHUNK), CHUNK)
        to = jnp.clip(col + (1 if side else -1), 0, n_col - 1)
        return pltpu.make_async_remote_copy(
            src_ref=w_ref.at[rows] if src is None else wg.at[b, rows],
            dst_ref=wg.at[b, rows],
            send_sem=w_send.at[side, b, h],
            recv_sem=w_recv.at[b, h],
            device_id={"col": to},
            device_id_type=MESH,
        )

    def send_own(h, c):
        @pl.when(col > 0)
        def _():
            w_copy(None, col, h, 0).start()

        @pl.when(col < n_col - 1)
        def _():
            w_copy(None, col, h, 1).start()

        return c

    lax.fori_loop(0, n_ch, send_own, 0)

    def t_copy(o):
        return pltpu.make_async_remote_copy(
            src_ref=t_ref,
            dst_ref=tg.at[row],
            send_sem=t_send.at[o - 1],
            recv_sem=t_recv.at[o - 1],
            device_id={"row": row_peer(o)},
            device_id_type=MESH,
        )

    if not gathered:
        for o in range(1, n_row):
            t_copy(o).start()
        t_own = pltpu.make_async_copy(t_ref, tg.at[row], own_sem.at[1])
    else:
        t_own = pltpu.make_async_copy(t_ref, tg, own_sem.at[1])
    t_own.start()
    w_own = pltpu.make_async_copy(w_ref, wg.at[col], own_sem.at[0])
    w_own.start()

    def place(src, which, q, first, last):
        i_count, j_local, kc = t_ref.shape
        i_out = i_count // n_depth
        per_r = j_local // n_row
        order = order_ref[...]

        def body(d, c):
            x = src[q, pl.ds(d * i_out, i_out)].reshape(i_out * j_local, kc)
            base = (d % n_lo) * rows_lo + (d // n_lo) * rows_d
            for x_part, into in zip(halves(x), (th, tl)):
                y = jnp.dot(order, x_part, preferred_element_type=jnp.float32).astype(jnp.bfloat16)
                for piece in range(n_row * i_out):
                    at = base + piece * (per_r * n_row) + q * per_r
                    into[which, pl.ds(pl.multiple_of(at, per_r), per_r), :] = y[piece * per_r : (piece + 1) * per_r]
            return c

        lax.fori_loop(first, last, body, 0)

    def plain(src, which, first, last):
        def body(m, c):
            at = pl.ds(pl.multiple_of(m * 64, 64), 64)
            th[which, at, :], tl[which, at, :] = halves(src[at, :])
            return c

        lax.fori_loop(first * (rows_all // 64) // n_depth, last * (rows_all // 64) // n_depth, body, 0)

    piece = t_ref.shape[0] // n_depth

    def e_copy(p):
        rows = pl.ds(p * piece, piece)
        return pltpu.make_async_remote_copy(
            src_ref=t_ref.at[rows],
            dst_ref=tg2.at[rows] if gathered else tg2.at[row, rows],
            send_sem=e_send.at[p],
            recv_sem=e_recv.at[p],
            device_id={"col": help_col},
            device_id_type=MESH,
        )

    def x_copy(p, o):
        rows = pl.ds(p * piece, piece)
        return pltpu.make_async_remote_copy(
            src_ref=tg2.at[row, rows],
            dst_ref=tg2.at[row, rows],
            send_sem=x_send.at[p, o - 1],
            recv_sem=x_recv.at[p, o - 1],
            device_id={"row": row_peer(o)},
            device_id_type=MESH,
        )

    def take(p):
        e_copy(p).wait_recv()
        if gathered:
            plain(tg2, 1, p, p + 1)
        else:
            for o in range(1, n_row):
                x_copy(p, o).start()
            place(tg2, 1, row, p, p + 1)

    def take_peers(p):
        if not gathered:
            for o in range(1, n_row):
                x_copy(p, o).wait_recv()
                place(tg2, 1, (row + n_row - o) % n_row, p, p + 1)

    t_own.wait()
    if not gathered:
        place(tg, 0, row, 0, n_depth)
    else:
        plain(tg, 0, 0, n_depth)

    def goes_right(b):
        return (col < n_col - 1) & ((b > 0) | (col < n_col - 2))

    def goes_left(b):
        return (col > 0) & ((b < n_col - 1) | (col > 1))

    def forward(b, h):
        w_copy(wg, b, h, 0).wait_recv()

        @pl.when((b < col) & goes_right(b))
        def _():
            w_copy(wg, b, h, 1).start()

        @pl.when((b > col) & goes_left(b))
        def _():
            w_copy(wg, b, h, 0).start()

    def first(h, c):
        @pl.when(col > 0)
        def _():
            forward(col - 1, h)

        @pl.when(col < n_col - 1)
        def _():
            forward(col + 1, h)

        return c

    lax.fori_loop(0, n_ch, first, 0)

    if not gathered:
        for o in range(1, n_row):
            t_copy(o).wait_recv()
            place(tg, 0, (row + n_row - o) % n_row, 0, n_depth)
    w_own.wait()

    @pl.when(at_end)
    def _():
        for p in range(n_depth):
            e_copy(p).start()

    near = jnp.minimum(col, n_col - 1 - col)

    def block_at(k):
        p, h = k // n_ch, k % n_ch
        both = p <= 2 * near
        s = jnp.where(both, (p + 1) // 2, p - near)
        left = jnp.where(both, p % 2 == 1, col > near)
        b = jnp.where(p == 0, col, jnp.where(left, col - s, col + s))
        return jnp.where(p < n_col, b, far), h, s

    def s1_copy(k):
        return pltpu.make_async_remote_copy(
            src_ref=part.at[k, pl.ds(pl.multiple_of((1 - lo) * rows_lo, rows_lo), rows_lo)],
            dst_ref=recv1.at[k],
            send_sem=s1_send.at[k],
            recv_sem=s1_recv.at[k],
            device_id={"depth": mate},
            device_id_type=MESH,
        )

    def s2_copy(k, o):
        return pltpu.make_async_remote_copy(
            src_ref=part.at[k, pl.ds(pl.multiple_of(lo * rows_lo + hi_peer(o) * rows_d, rows_d), rows_d)],
            dst_ref=recv2.at[k, o - 1],
            send_sem=s2_send.at[k, o - 1],
            recv_sem=s2_recv.at[k, o - 1],
            device_id={"depth": hi_peer(o) * n_lo + lo},
            device_id_type=MESH,
        )

    def out_cols(k):
        b, h, _ = block_at(k)
        return pl.ds(pl.multiple_of((row * n_col + b) * ab_rows + h * CHUNK, CHUNK), CHUNK)

    def r_copy(k, o):
        return pltpu.make_async_remote_copy(
            src_ref=fin.at[k, pl.ds(pl.multiple_of(row_peer(o) * rows_r, rows_r), rows_r)],
            dst_ref=out_ref.at[:, out_cols(k)],
            send_sem=r_send.at[k, o - 1],
            recv_sem=r_recv.at[k, o - 1],
            device_id={"row": row_peer(o)},
            device_id_type=MESH,
        )

    def d_copy(k, o):
        h = k % n_ch
        return pltpu.make_async_remote_copy(
            src_ref=fin.at[k, pl.ds(pl.multiple_of(row_peer(o) * rows_r, rows_r), rows_r)],
            dst_ref=out_ref.at[:, out_cols(k)],
            send_sem=d_send.at[h, o],
            recv_sem=d_recv.at[h, o],
            device_id={"row": row_peer(o), "col": end_col},
            device_id_type=MESH,
        )

    def dot(a, b):
        return lax.dot_general(a, b, (((1,), (1,)), ((), ())), preferred_element_type=jnp.float32)

    def step(k, c):
        h_now = k % n_ch
        per_h = n_depth // n_ch

        @pl.when(helps & (k >= steps - n_ch) & (k < steps))
        def _():
            for p in range(per_h):

                @pl.when(h_now > 0)
                def _():
                    take_peers((h_now - 1) * per_h + p)

                take(h_now * per_h + p)

        @pl.when(helps & (k == steps))
        def _():
            for p in range(per_h):
                take_peers((n_ch - 1) * per_h + p)

        @pl.when(k < total_steps)
        def _():
            b, h, s = block_at(k)
            which = jnp.where(k < steps, 0, 1)

            @pl.when((s >= 2) & (k < steps))
            def _():
                forward(b, h)

            wh, wl = halves(wg[b, pl.ds(pl.multiple_of(h * CHUNK, CHUNK), CHUNK), :])
            tile = rows_all // 2
            for m in range(2):
                at = pl.ds(m * tile, tile)
                a = th[which, at, :]
                part[k, at, :] = dot(a, wh) + dot(a, wl) + dot(tl[which, at, :], wh)
            s1_copy(k).start()

        @pl.when((k >= 1) & (k < total_steps + 1))
        def _():
            j = k - 1
            s1_copy(j).wait_recv()
            at = pl.ds(pl.multiple_of(lo * rows_lo, rows_lo), rows_lo)
            part[j, at, :] = part[j, at, :] + recv1[j]
            for o in range(1, n_hi):
                s2_copy(j, o).start()

        @pl.when(k >= 2)
        def _():
            j = k - 2
            total = part[j, pl.ds(pl.multiple_of(lo * rows_lo + hi * rows_d, rows_d), rows_d), :]
            for o in range(1, n_hi):
                s2_copy(j, o).wait_recv()
                total = total + recv2[j, o - 1]
            fin[j] = total

            @pl.when(j < normal)
            def _():
                for o in range(1, n_row):
                    r_copy(j, o).start()
                out_ref[:, out_cols(j)] = fin[j, pl.ds(pl.multiple_of(row * rows_r, rows_r), rows_r), :]

            @pl.when(j >= normal)
            def _():
                for o in range(n_row):
                    d_copy(j, o).start()

        return c

    lax.fori_loop(0, total_steps + 2, step, 0)

    def drain(k, c):
        s1_copy(k).wait_send()
        for o in range(1, n_hi):
            s2_copy(k, o).wait_send()

        @pl.when(k < normal)
        def _():
            for o in range(1, n_row):
                r_copy(k, o).wait_send()
                r_copy(k, o).wait_recv()

        @pl.when(k >= normal)
        def _():
            for o in range(n_row):
                d_copy(k, o).wait_send()

        return c

    lax.fori_loop(0, total_steps, drain, 0)

    def drain_w(k, c):
        b, h = k // n_ch, k % n_ch

        @pl.when((b <= col) & goes_right(b))
        def _():
            w_copy(wg, b, h, 1).wait_send()

        @pl.when((b >= col) & goes_left(b))
        def _():
            w_copy(wg, b, h, 0).wait_send()

        return c

    lax.fori_loop(0, steps, drain_w, 0)

    @pl.when(at_end)
    def _():
        for p in range(n_depth):
            e_copy(p).wait_send()
        for h in range(n_ch):
            for o in range(n_row):
                d_copy(h, o).wait_recv()

    if not gathered:

        @pl.when(helps)
        def _():
            for p in range(n_depth):
                for o in range(1, n_row):
                    x_copy(p, o).wait_send()

    if not gathered:
        for o in range(1, n_row):
            t_copy(o).wait_send()


def shards(sizes, integrals, amplitudes):
    n_row, n_col, n_depth = sizes
    n_lo = LANES
    n_hi = n_depth // n_lo
    kc, i_count, j_local = amplitudes.shape
    j_count = j_local * n_row
    ab_rows = integrals.shape[0]
    n_ch = ab_rows // CHUNK
    slots = (n_col + 1) * n_ch
    rows_all = i_count * j_count
    rows_lo = rows_all // n_lo
    rows_d = rows_lo // n_hi
    rows_r = rows_d // n_row
    i_out = i_count // n_depth
    gathered = j_local % (16 * n_row) != 0
    side = i_out * j_local
    tiny = j_local if gathered else n_row
    source = np.arange(side).reshape(i_out, j_local // tiny, tiny).transpose(2, 0, 1).reshape(-1)
    order = jnp.asarray(np.eye(side)[source], jnp.bfloat16)
    t = jnp.transpose(amplitudes, (1, 2, 0))
    if gathered:
        t = lax.all_gather(t, "row", axis=1, tiled=True)
        t = t.reshape(n_hi, n_lo, i_out, j_count // n_row, n_row, kc)
        t = jnp.transpose(t, (1, 0, 4, 2, 3, 5)).reshape(rows_all, kc)
        tg = pltpu.VMEM(t.shape, jnp.float32)
    else:
        tg = pltpu.VMEM((n_row,) + t.shape, jnp.float32)
    dma = pltpu.SemaphoreType.DMA
    out = pl.pallas_call(
        functools.partial(kernel, sizes, gathered),
        out_shape=jax.ShapeDtypeStruct((rows_r, n_row * n_col * ab_rows), jnp.float32),
        in_specs=[pl.BlockSpec(memory_space=pl.ANY)] * 2 + [pl.BlockSpec(memory_space=pltpu.VMEM)],
        out_specs=pl.BlockSpec(memory_space=pltpu.VMEM),
        scratch_shapes=[
            pltpu.VMEM((n_col, ab_rows, kc), jnp.float32),
            tg,
            tg,
            pltpu.VMEM((2, rows_all, kc), jnp.bfloat16),
            pltpu.VMEM((2, rows_all, kc), jnp.bfloat16),
            pltpu.VMEM((slots, rows_all, CHUNK), jnp.float32),
            pltpu.VMEM((slots, rows_lo, CHUNK), jnp.float32),
            pltpu.VMEM((slots, max(n_hi - 1, 1), rows_d, CHUNK), jnp.float32),
            pltpu.VMEM((slots, rows_d, CHUNK), jnp.float32),
            dma((2,)),
            dma((2, n_col, ab_rows // CHUNK)),
            dma((n_col, ab_rows // CHUNK)),
            dma((max(n_row - 1, 1),)),
            dma((max(n_row - 1, 1),)),
            dma((slots,)),
            dma((slots,)),
            dma((slots, max(n_hi - 1, 1))),
            dma((slots, max(n_hi - 1, 1))),
            dma((slots, max(n_row - 1, 1))),
            dma((slots, max(n_row - 1, 1))),
            dma((n_depth,)),
            dma((n_depth,)),
            dma((n_depth, max(n_row - 1, 1))),
            dma((n_depth, max(n_row - 1, 1))),
            dma((n_ch, n_row)),
            dma((n_ch, n_row)),
        ],
        compiler_params=pltpu.CompilerParams(
            collective_id=0, has_side_effects=True, vmem_limit_bytes=60 * 2**20
        ),
        cost_estimate=pl.CostEstimate(
            flops=6 * rows_all * kc * ab_rows * n_col, bytes_accessed=6 * 2**20, transcendentals=0
        ),
    )(integrals, t, order)
    return out.reshape(i_out, j_count // n_row, n_row * n_col * ab_rows)


def solution(mesh):
    sizes = (mesh.shape["row"], mesh.shape["col"], mesh.shape["depth"])
    placed = (P(("row", "col"), "depth"), P("depth", "col", "row"))
    return jax.shard_map(
        functools.partial(shards, sizes),
        mesh=mesh,
        in_specs=placed,
        out_specs=P(("col", "depth"), "row", None),
        check_vma=False,
    )
```

```python
import functools

import jax
import jax.numpy as jnp
import numpy as np
from jax import lax
from jax.experimental import pallas as pl
from jax.experimental.pallas import tpu as pltpu
from jax.sharding import PartitionSpec as P

MESH = pl.DeviceIdType.MESH
CHUNK = 256
LANES = 2


def halves(x):
    hi = x.astype(jnp.bfloat16)
    lo = (x - hi.astype(jnp.float32)).astype(jnp.bfloat16)
    return hi, lo


def kernel(sizes, gathered, w_ref, t_ref, order_ref, out_ref, wg, tg, tg2, th, tl, part, recv1, recv2, fin,
           own_sem, w_send, w_recv, t_send, t_recv, s1_send, s1_recv, s2_send, s2_recv, r_send, r_recv,
           e_send, e_recv, x_send, x_recv, d_send, d_recv):
    n_row, n_col, n_depth = sizes
    n_lo = LANES
    n_hi = n_depth // n_lo
    ab_rows = w_ref.shape[0]
    n_ch = ab_rows // CHUNK
    assert n_ch == 2 and n_depth == 4 and n_col == 4
    steps = n_col * n_ch
    rows_all = th.shape[1]
    rows_lo = rows_all // n_lo
    rows_d = rows_lo // n_hi
    rows_r = rows_d // n_row
    row, col, depth = lax.axis_index("row"), lax.axis_index("col"), lax.axis_index("depth")
    hi, lo = depth // n_lo, depth % n_lo

    def row_peer(o):
        return (row + o) % n_row

    def hi_peer(o):
        return (hi + o) % n_hi

    mate = hi * n_lo + (1 - lo)
    at_end = (col == 0) | (col == n_col - 1)
    helps = (col == 1) | (col == n_col - 2)
    far = jnp.where(col < n_col // 2, n_col - 1, 0)
    end_col = jnp.where(col < n_col // 2, 0, n_col - 1)
    help_col = jnp.where(col < n_col // 2, 1, n_col - 2)
    normal = jnp.where(at_end, steps - n_ch, steps)
    total_steps = jnp.where(helps, steps + n_ch, normal)

    barrier = pltpu.get_barrier_semaphore()
    for o in range(1, n_row):
        pl.semaphore_signal(barrier, inc=1, device_id={"row": row_peer(o)}, device_id_type=MESH)
    pl.semaphore_signal(barrier, inc=1, device_id={"depth": mate}, device_id_type=MESH)
    for o in range(1, n_hi):
        pl.semaphore_signal(barrier, inc=1, device_id={"depth": hi_peer(o) * n_lo + lo}, device_id_type=MESH)

    @pl.when(col > 0)
    def _():
        pl.semaphore_signal(barrier, inc=1, device_id={"col": col - 1}, device_id_type=MESH)

    @pl.when(col < n_col - 1)
    def _():
        pl.semaphore_signal(barrier, inc=1, device_id={"col": col + 1}, device_id_type=MESH)

    for o in range(1, n_row):

        @pl.when(at_end)
        def _():
            pl.semaphore_signal(
                barrier, inc=1, device_id={"row": row_peer(o), "col": help_col}, device_id_type=MESH
            )

        @pl.when(helps)
        def _():
            pl.semaphore_signal(
                barrier, inc=1, device_id={"row": row_peer(o), "col": end_col}, device_id_type=MESH
            )

    fixed = (n_row - 1) + 1 + (n_hi - 1)
    ends = jnp.where(col > 0, 1, 0) + jnp.where(col < n_col - 1, 1, 0)
    diagonal = jnp.where(at_end | helps, n_row - 1, 0)
    pl.semaphore_wait(barrier, fixed + ends + diagonal)

    def w_copy(src, b, h, side):
        rows = pl.ds(pl.multiple_of(h * CHUNK, CHUNK), CHUNK)
        to = jnp.clip(col + (1 if side else -1), 0, n_col - 1)
        return pltpu.make_async_remote_copy(
            src_ref=w_ref.at[rows] if src is None else wg.at[b, rows],
            dst_ref=wg.at[b, rows],
            send_sem=w_send.at[side, b, h],
            recv_sem=w_recv.at[b, h],
            device_id={"col": to},
            device_id_type=MESH,
        )

    def own_sends(act, h):
        @pl.when(col > 0)
        def _():
            getattr(w_copy(None, col, h, 0), act)()

        @pl.when(col < n_col - 1)
        def _():
            getattr(w_copy(None, col, h, 1), act)()

    def near_sends(act, h):
        @pl.when((col > 0) & goes_right(col - 1))
        def _():
            getattr(w_copy(wg, col - 1, h, 1), act)()

        @pl.when((col < n_col - 1) & goes_left(col + 1))
        def _():
            getattr(w_copy(wg, col + 1, h, 0), act)()

    def near_arrive(h):
        @pl.when(col > 0)
        def _():
            w_copy(wg, col - 1, h, 0).wait_recv()

        @pl.when(col < n_col - 1)
        def _():
            w_copy(wg, col + 1, h, 0).wait_recv()

    def goes_right(b):
        return (col < n_col - 1) & ((b > 0) | (col < n_col - 2))

    def goes_left(b):
        return (col > 0) & ((b < n_col - 1) | (col > 1))

    own_sends("start", 0)

    def t_copy(o):
        return pltpu.make_async_remote_copy(
            src_ref=t_ref,
            dst_ref=tg.at[row],
            send_sem=t_send.at[o - 1],
            recv_sem=t_recv.at[o - 1],
            device_id={"row": row_peer(o)},
            device_id_type=MESH,
        )

    if not gathered:
        for o in range(1, n_row):
            t_copy(o).start()
        t_own = pltpu.make_async_copy(t_ref, tg.at[row], own_sem.at[1])
    else:
        t_own = pltpu.make_async_copy(t_ref, tg, own_sem.at[1])
    t_own.start()
    w_own = pltpu.make_async_copy(w_ref, wg.at[col], own_sem.at[0])
    w_own.start()

    def place(src, which, q, first, last):
        i_count, j_local, kc = t_ref.shape
        i_out = i_count // n_depth
        per_r = j_local // n_row
        order = order_ref[...]

        def body(d, c):
            x = src[q, pl.ds(d * i_out, i_out)].reshape(i_out * j_local, kc)
            base = (d % n_lo) * rows_lo + (d // n_lo) * rows_d
            for x_part, into in zip(halves(x), (th, tl)):
                y = jnp.dot(order, x_part, preferred_element_type=jnp.float32).astype(jnp.bfloat16)
                for piece in range(n_row * i_out):
                    at = base + piece * (per_r * n_row) + q * per_r
                    into[which, pl.ds(pl.multiple_of(at, per_r), per_r), :] = y[piece * per_r : (piece + 1) * per_r]
            return c

        lax.fori_loop(first, last, body, 0)

    def plain(src, which, first, last):
        def body(m, c):
            at = pl.ds(pl.multiple_of(m * 64, 64), 64)
            th[which, at, :], tl[which, at, :] = halves(src[at, :])
            return c

        lax.fori_loop(first * (rows_all // 64) // n_depth, last * (rows_all // 64) // n_depth, body, 0)

    piece = t_ref.shape[0] // n_depth

    def e_copy(p):
        rows = pl.ds(p * piece, piece)
        return pltpu.make_async_remote_copy(
            src_ref=t_ref.at[rows],
            dst_ref=tg2.at[rows] if gathered else tg2.at[row, rows],
            send_sem=e_send.at[p],
            recv_sem=e_recv.at[p],
            device_id={"col": help_col},
            device_id_type=MESH,
        )

    def x_copy(p, o):
        rows = pl.ds(p * piece, piece)
        return pltpu.make_async_remote_copy(
            src_ref=tg2.at[row, rows],
            dst_ref=tg2.at[row, rows],
            send_sem=x_send.at[p, o - 1],
            recv_sem=x_recv.at[p, o - 1],
            device_id={"row": row_peer(o)},
            device_id_type=MESH,
        )

    def take(p):
        e_copy(p).wait_recv()
        if gathered:
            plain(tg2, 1, p, p + 1)
        else:
            for o in range(1, n_row):
                x_copy(p, o).start()
            place(tg2, 1, row, p, p + 1)

    def take_peers(p):
        if not gathered:
            for o in range(1, n_row):
                x_copy(p, o).wait_recv()
                place(tg2, 1, (row + n_row - o) % n_row, p, p + 1)

    t_own.wait()
    if not gathered:
        place(tg, 0, row, 0, n_depth)
    else:
        plain(tg, 0, 0, n_depth)

    own_sends("wait_send", 0)
    own_sends("start", 1)
    near_arrive(0)
    own_sends("wait_send", 1)
    near_sends("start", 0)

    @pl.when(at_end)
    def _():
        e_copy(0).start()

    near_arrive(1)
    if not gathered:
        for o in range(1, n_row):
            t_copy(o).wait_recv()
            place(tg, 0, (row + n_row - o) % n_row, 0, n_depth)
    w_own.wait()

    near = jnp.minimum(col, n_col - 1 - col)

    def block_at(k):
        p, h = k // n_ch, k % n_ch
        both = p <= 2 * near
        s = jnp.where(both, (p + 1) // 2, p - near)
        left = jnp.where(both, p % 2 == 1, col > near)
        b = jnp.where(p == 0, col, jnp.where(left, col - s, col + s))
        return jnp.where(p < n_col, b, far), h, s

    def s1_copy(k):
        return pltpu.make_async_remote_copy(
            src_ref=part.at[k, pl.ds(pl.multiple_of((1 - lo) * rows_lo, rows_lo), rows_lo)],
            dst_ref=recv1.at[k],
            send_sem=s1_send.at[k],
            recv_sem=s1_recv.at[k],
            device_id={"depth": mate},
            device_id_type=MESH,
        )

    def s2_copy(k, o):
        return pltpu.make_async_remote_copy(
            src_ref=part.at[k, pl.ds(pl.multiple_of(lo * rows_lo + hi_peer(o) * rows_d, rows_d), rows_d)],
            dst_ref=recv2.at[k, o - 1],
            send_sem=s2_send.at[k, o - 1],
            recv_sem=s2_recv.at[k, o - 1],
            device_id={"depth": hi_peer(o) * n_lo + lo},
            device_id_type=MESH,
        )

    def out_cols(k):
        b, h, _ = block_at(k)
        return pl.ds(pl.multiple_of((row * n_col + b) * ab_rows + h * CHUNK, CHUNK), CHUNK)

    def r_copy(k, o):
        return pltpu.make_async_remote_copy(
            src_ref=fin.at[k, pl.ds(pl.multiple_of(row_peer(o) * rows_r, rows_r), rows_r)],
            dst_ref=out_ref.at[:, out_cols(k)],
            send_sem=r_send.at[k, o - 1],
            recv_sem=r_recv.at[k, o - 1],
            device_id={"row": row_peer(o)},
            device_id_type=MESH,
        )

    def d_copy(k, o):
        h = k % n_ch
        return pltpu.make_async_remote_copy(
            src_ref=fin.at[k, pl.ds(pl.multiple_of(row_peer(o) * rows_r, rows_r), rows_r)],
            dst_ref=out_ref.at[:, out_cols(k)],
            send_sem=d_send.at[h, o],
            recv_sem=d_recv.at[h, o],
            device_id={"row": row_peer(o), "col": end_col},
            device_id_type=MESH,
        )

    def dot(a, b):
        return lax.dot_general(a, b, (((1,), (1,)), ((), ())), preferred_element_type=jnp.float32)

    def step(k, c):
        h_now = k % n_ch
        per_h = n_depth // n_ch

        @pl.when(helps & (k >= steps - n_ch) & (k < steps))
        def _():
            for p in range(per_h):

                @pl.when(h_now > 0)
                def _():
                    take_peers((h_now - 1) * per_h + p)

                take(h_now * per_h + p)

        @pl.when(helps & (k == steps))
        def _():
            for p in range(per_h):
                take_peers((n_ch - 1) * per_h + p)

        @pl.when(k < total_steps)
        def _():
            b, h, s = block_at(k)
            which = jnp.where(k < steps, 0, 1)

            late = k - (normal - n_ch)

            @pl.when(at_end & (late == 0))
            def _():
                e_copy(0).wait_send()
                e_copy(1).start()

            @pl.when(at_end & (late == 1))
            def _():
                e_copy(2).wait_send()
                e_copy(3).start()

            @pl.when((s >= 2) & (k < steps))
            def _():
                w_copy(wg, b, h, 0).wait_recv()

            @pl.when(late == 0)
            def _():
                near_sends("wait_send", 0)
                near_sends("start", 1)

                @pl.when(at_end)
                def _():
                    e_copy(1).wait_send()
                    e_copy(2).start()


            wh, wl = halves(wg[b, pl.ds(pl.multiple_of(h * CHUNK, CHUNK), CHUNK), :])
            tile = rows_all // 2
            for m in range(2):
                at = pl.ds(m * tile, tile)
                a = th[which, at, :]
                part[k, at, :] = dot(a, wh) + dot(a, wl) + dot(tl[which, at, :], wh)
            s1_copy(k).start()

        @pl.when((k >= 1) & (k < total_steps + 1))
        def _():
            j = k - 1
            s1_copy(j).wait_recv()
            at = pl.ds(pl.multiple_of(lo * rows_lo, rows_lo), rows_lo)
            part[j, at, :] = part[j, at, :] + recv1[j]
            for o in range(1, n_hi):
                s2_copy(j, o).start()

        @pl.when(k >= 2)
        def _():
            j = k - 2
            total = part[j, pl.ds(pl.multiple_of(lo * rows_lo + hi * rows_d, rows_d), rows_d), :]
            for o in range(1, n_hi):
                s2_copy(j, o).wait_recv()
                total = total + recv2[j, o - 1]
            fin[j] = total

            @pl.when(j < normal)
            def _():
                for o in range(1, n_row):
                    r_copy(j, o).start()
                out_ref[:, out_cols(j)] = fin[j, pl.ds(pl.multiple_of(row * rows_r, rows_r), rows_r), :]

            @pl.when(j >= normal)
            def _():
                for o in range(n_row):
                    d_copy(j, o).start()

        return c

    lax.fori_loop(0, total_steps + 2, step, 0)

    def drain(k, c):
        s1_copy(k).wait_send()
        for o in range(1, n_hi):
            s2_copy(k, o).wait_send()

        @pl.when(k < normal)
        def _():
            for o in range(1, n_row):
                r_copy(k, o).wait_send()
                r_copy(k, o).wait_recv()

        @pl.when(k >= normal)
        def _():
            for o in range(n_row):
                d_copy(k, o).wait_send()

        return c

    lax.fori_loop(0, total_steps, drain, 0)

    near_sends("wait_send", 1)

    @pl.when(at_end)
    def _():
        e_copy(3).wait_send()
        for h in range(n_ch):
            for o in range(n_row):
                d_copy(h, o).wait_recv()

    if not gathered:

        @pl.when(helps)
        def _():
            for p in range(n_depth):
                for o in range(1, n_row):
                    x_copy(p, o).wait_send()

    if not gathered:
        for o in range(1, n_row):
            t_copy(o).wait_send()


def shards(sizes, integrals, amplitudes):
    n_row, n_col, n_depth = sizes
    n_lo = LANES
    n_hi = n_depth // n_lo
    kc, i_count, j_local = amplitudes.shape
    j_count = j_local * n_row
    ab_rows = integrals.shape[0]
    n_ch = ab_rows // CHUNK
    slots = (n_col + 1) * n_ch
    rows_all = i_count * j_count
    rows_lo = rows_all // n_lo
    rows_d = rows_lo // n_hi
    rows_r = rows_d // n_row
    i_out = i_count // n_depth
    gathered = j_local % (16 * n_row) != 0
    side = i_out * j_local
    tiny = j_local if gathered else n_row
    source = np.arange(side).reshape(i_out, j_local // tiny, tiny).transpose(2, 0, 1).reshape(-1)
    order = jnp.asarray(np.eye(side)[source], jnp.bfloat16)
    t = jnp.transpose(amplitudes, (1, 2, 0))
    if gathered:
        t = lax.all_gather(t, "row", axis=1, tiled=True)
        t = t.reshape(n_hi, n_lo, i_out, j_count // n_row, n_row, kc)
        t = jnp.transpose(t, (1, 0, 4, 2, 3, 5)).reshape(rows_all, kc)
        tg = pltpu.VMEM(t.shape, jnp.float32)
    else:
        tg = pltpu.VMEM((n_row,) + t.shape, jnp.float32)
    dma = pltpu.SemaphoreType.DMA
    out = pl.pallas_call(
        functools.partial(kernel, sizes, gathered),
        out_shape=jax.ShapeDtypeStruct((rows_r, n_row * n_col * ab_rows), jnp.float32),
        in_specs=[pl.BlockSpec(memory_space=pl.ANY)] * 2 + [pl.BlockSpec(memory_space=pltpu.VMEM)],
        out_specs=pl.BlockSpec(memory_space=pltpu.VMEM),
        scratch_shapes=[
            pltpu.VMEM((n_col, ab_rows, kc), jnp.float32),
            tg,
            tg,
            pltpu.VMEM((2, rows_all, kc), jnp.bfloat16),
            pltpu.VMEM((2, rows_all, kc), jnp.bfloat16),
            pltpu.VMEM((slots, rows_all, CHUNK), jnp.float32),
            pltpu.VMEM((slots, rows_lo, CHUNK), jnp.float32),
            pltpu.VMEM((slots, max(n_hi - 1, 1), rows_d, CHUNK), jnp.float32),
            pltpu.VMEM((slots, rows_d, CHUNK), jnp.float32),
            dma((2,)),
            dma((2, n_col, ab_rows // CHUNK)),
            dma((n_col, ab_rows // CHUNK)),
            dma((max(n_row - 1, 1),)),
            dma((max(n_row - 1, 1),)),
            dma((slots,)),
            dma((slots,)),
            dma((slots, max(n_hi - 1, 1))),
            dma((slots, max(n_hi - 1, 1))),
            dma((slots, max(n_row - 1, 1))),
            dma((slots, max(n_row - 1, 1))),
            dma((n_depth,)),
            dma((n_depth,)),
            dma((n_depth, max(n_row - 1, 1))),
            dma((n_depth, max(n_row - 1, 1))),
            dma((n_ch, n_row)),
            dma((n_ch, n_row)),
        ],
        compiler_params=pltpu.CompilerParams(
            collective_id=0, has_side_effects=True, vmem_limit_bytes=60 * 2**20
        ),
        cost_estimate=pl.CostEstimate(
            flops=6 * rows_all * kc * ab_rows * n_col, bytes_accessed=6 * 2**20, transcendentals=0
        ),
    )(integrals, t, order)
    return out.reshape(i_out, j_count // n_row, n_row * n_col * ab_rows)


def solution(mesh):
    sizes = (mesh.shape["row"], mesh.shape["col"], mesh.shape["depth"])
    placed = (P(("row", "col"), "depth"), P("depth", "col", "row"))
    return jax.shard_map(
        functools.partial(shards, sizes),
        mesh=mesh,
        in_specs=placed,
        out_specs=P(("col", "depth"), "row", None),
        check_vma=False,
    )
```

```python
import functools

import jax
import jax.numpy as jnp
import numpy as np
from jax import lax
from jax.experimental import pallas as pl
from jax.experimental.pallas import tpu as pltpu
from jax.sharding import PartitionSpec as P

MESH = pl.DeviceIdType.MESH
CHUNK = 256
LANES = 2


def halves(x):
    hi = x.astype(jnp.bfloat16)
    lo = (x - hi.astype(jnp.float32)).astype(jnp.bfloat16)
    return hi, lo


def kernel(sizes, gathered, w_ref, t_ref, order_ref, out_ref, wg, tg, tg2, th, tl, part, recv1, recv2, fin,
           own_sem, w_send, w_recv, t_send, t_recv, s1_send, s1_recv, s2_send, s2_recv, r_send, r_recv,
           e_send, e_recv, x_send, x_recv, d_send, d_recv):
    n_row, n_col, n_depth = sizes
    n_lo = LANES
    n_hi = n_depth // n_lo
    ab_rows = w_ref.shape[0]
    n_ch = ab_rows // CHUNK
    assert n_ch == 2 and n_depth == 4 and n_col == 4
    steps = n_col * n_ch
    rows_all = th.shape[1]
    rows_lo = rows_all // n_lo
    rows_d = rows_lo // n_hi
    rows_r = rows_d // n_row
    row, col, depth = lax.axis_index("row"), lax.axis_index("col"), lax.axis_index("depth")
    hi, lo = depth // n_lo, depth % n_lo

    def row_peer(o):
        return (row + o) % n_row

    def hi_peer(o):
        return (hi + o) % n_hi

    mate = hi * n_lo + (1 - lo)
    at_end = (col == 0) | (col == n_col - 1)
    helps = (col == 1) | (col == n_col - 2)
    far = jnp.where(col < n_col // 2, n_col - 1, 0)
    end_col = jnp.where(col < n_col // 2, 0, n_col - 1)
    help_col = jnp.where(col < n_col // 2, 1, n_col - 2)
    normal = jnp.where(at_end, steps - n_ch, steps)
    total_steps = jnp.where(helps, steps + n_ch, normal)

    barrier = pltpu.get_barrier_semaphore()
    for o in range(1, n_row):
        pl.semaphore_signal(barrier, inc=1, device_id={"row": row_peer(o)}, device_id_type=MESH)
    pl.semaphore_signal(barrier, inc=1, device_id={"depth": mate}, device_id_type=MESH)
    for o in range(1, n_hi):
        pl.semaphore_signal(barrier, inc=1, device_id={"depth": hi_peer(o) * n_lo + lo}, device_id_type=MESH)

    @pl.when(col > 0)
    def _():
        pl.semaphore_signal(barrier, inc=1, device_id={"col": col - 1}, device_id_type=MESH)

    @pl.when(col < n_col - 1)
    def _():
        pl.semaphore_signal(barrier, inc=1, device_id={"col": col + 1}, device_id_type=MESH)

    for o in range(1, n_row):

        @pl.when(at_end)
        def _():
            pl.semaphore_signal(
                barrier, inc=1, device_id={"row": row_peer(o), "col": help_col}, device_id_type=MESH
            )

        @pl.when(helps)
        def _():
            pl.semaphore_signal(
                barrier, inc=1, device_id={"row": row_peer(o), "col": end_col}, device_id_type=MESH
            )

    fixed = (n_row - 1) + 1 + (n_hi - 1)
    ends = jnp.where(col > 0, 1, 0) + jnp.where(col < n_col - 1, 1, 0)
    diagonal = jnp.where(at_end | helps, n_row - 1, 0)
    pl.semaphore_wait(barrier, fixed + ends + diagonal)

    def w_copy(src, b, h, side):
        rows = pl.ds(pl.multiple_of(h * CHUNK, CHUNK), CHUNK)
        to = jnp.clip(col + (1 if side else -1), 0, n_col - 1)
        return pltpu.make_async_remote_copy(
            src_ref=w_ref.at[rows] if src is None else wg.at[b, rows],
            dst_ref=wg.at[b, rows],
            send_sem=w_send.at[side, b, h],
            recv_sem=w_recv.at[b, h],
            device_id={"col": to},
            device_id_type=MESH,
        )

    def own_sends(act, h):
        @pl.when(col > 0)
        def _():
            getattr(w_copy(None, col, h, 0), act)()

        @pl.when(col < n_col - 1)
        def _():
            getattr(w_copy(None, col, h, 1), act)()

    def near_sends(act, h):
        @pl.when((col > 0) & goes_right(col - 1))
        def _():
            getattr(w_copy(wg, col - 1, h, 1), act)()

        @pl.when((col < n_col - 1) & goes_left(col + 1))
        def _():
            getattr(w_copy(wg, col + 1, h, 0), act)()

    def near_arrive(h):
        @pl.when(col > 0)
        def _():
            w_copy(wg, col - 1, h, 0).wait_recv()

        @pl.when(col < n_col - 1)
        def _():
            w_copy(wg, col + 1, h, 0).wait_recv()

    def goes_right(b):
        return (col < n_col - 1) & ((b > 0) | (col < n_col - 2))

    def goes_left(b):
        return (col > 0) & ((b < n_col - 1) | (col > 1))

    own_sends("start", 0)

    def t_copy(o):
        return pltpu.make_async_remote_copy(
            src_ref=t_ref,
            dst_ref=tg.at[row],
            send_sem=t_send.at[o - 1],
            recv_sem=t_recv.at[o - 1],
            device_id={"row": row_peer(o)},
            device_id_type=MESH,
        )

    if not gathered:
        for o in range(1, n_row):
            t_copy(o).start()
        t_own = pltpu.make_async_copy(t_ref, tg.at[row], own_sem.at[1])
    else:
        t_own = pltpu.make_async_copy(t_ref, tg, own_sem.at[1])
    t_own.start()
    w_own = pltpu.make_async_copy(w_ref, wg.at[col], own_sem.at[0])
    w_own.start()

    def place(src, which, q, first, last):
        i_count, j_local, kc = t_ref.shape
        i_out = i_count // n_depth
        per_r = j_local // n_row
        order = order_ref[...]

        def body(d, c):
            x = src[q, pl.ds(d * i_out, i_out)].reshape(i_out * j_local, kc)
            base = (d % n_lo) * rows_lo + (d // n_lo) * rows_d
            for x_part, into in zip(halves(x), (th, tl)):
                y = jnp.dot(order, x_part, preferred_element_type=jnp.float32).astype(jnp.bfloat16)
                for piece in range(n_row * i_out):
                    at = base + piece * (per_r * n_row) + q * per_r
                    into[which, pl.ds(pl.multiple_of(at, per_r), per_r), :] = y[piece * per_r : (piece + 1) * per_r]
            return c

        lax.fori_loop(first, last, body, 0)

    def plain(src, which, first, last):
        def body(m, c):
            at = pl.ds(pl.multiple_of(m * 64, 64), 64)
            th[which, at, :], tl[which, at, :] = halves(src[at, :])
            return c

        lax.fori_loop(first * (rows_all // 64) // n_depth, last * (rows_all // 64) // n_depth, body, 0)

    piece = t_ref.shape[0] // n_depth

    def e_copy(p):
        rows = pl.ds(p * piece, piece)
        return pltpu.make_async_remote_copy(
            src_ref=t_ref.at[rows],
            dst_ref=tg2.at[rows] if gathered else tg2.at[row, rows],
            send_sem=e_send.at[p],
            recv_sem=e_recv.at[p],
            device_id={"col": help_col},
            device_id_type=MESH,
        )

    def x_copy(p, o):
        rows = pl.ds(p * piece, piece)
        return pltpu.make_async_remote_copy(
            src_ref=tg2.at[row, rows],
            dst_ref=tg2.at[row, rows],
            send_sem=x_send.at[p, o - 1],
            recv_sem=x_recv.at[p, o - 1],
            device_id={"row": row_peer(o)},
            device_id_type=MESH,
        )

    def take(p):
        e_copy(p).wait_recv()
        if not gathered:
            for o in range(1, n_row):
                x_copy(p, o).start()

    def place_own(p):
        if gathered:
            plain(tg2, 1, p, p + 1)
        else:
            place(tg2, 1, row, p, p + 1)

    def place_peers(p):
        if not gathered:
            for o in range(1, n_row):
                x_copy(p, o).wait_recv()
                place(tg2, 1, (row + n_row - o) % n_row, p, p + 1)

    t_own.wait()
    if not gathered:
        place(tg, 0, row, 0, n_depth)
    else:
        plain(tg, 0, 0, n_depth)

    own_sends("wait_send", 0)
    own_sends("start", 1)
    near_arrive(0)
    own_sends("wait_send", 1)
    near_sends("start", 0)

    @pl.when(at_end)
    def _():
        e_copy(0).start()
        e_copy(1).start()

    near_arrive(1)
    if not gathered:
        for o in range(1, n_row):
            t_copy(o).wait_recv()
            place(tg, 0, (row + n_row - o) % n_row, 0, n_depth)
    w_own.wait()

    near = jnp.minimum(col, n_col - 1 - col)

    def block_at(k):
        p, h = k // n_ch, k % n_ch
        both = p <= 2 * near
        s = jnp.where(both, (p + 1) // 2, p - near)
        left = jnp.where(both, p % 2 == 1, col > near)
        b = jnp.where(p == 0, col, jnp.where(left, col - s, col + s))
        return jnp.where(p < n_col, b, far), h, s

    def s1_copy(k):
        return pltpu.make_async_remote_copy(
            src_ref=part.at[k, pl.ds(pl.multiple_of((1 - lo) * rows_lo, rows_lo), rows_lo)],
            dst_ref=recv1.at[k],
            send_sem=s1_send.at[k],
            recv_sem=s1_recv.at[k],
            device_id={"depth": mate},
            device_id_type=MESH,
        )

    def s2_copy(k, o):
        return pltpu.make_async_remote_copy(
            src_ref=part.at[k, pl.ds(pl.multiple_of(lo * rows_lo + hi_peer(o) * rows_d, rows_d), rows_d)],
            dst_ref=recv2.at[k, o - 1],
            send_sem=s2_send.at[k, o - 1],
            recv_sem=s2_recv.at[k, o - 1],
            device_id={"depth": hi_peer(o) * n_lo + lo},
            device_id_type=MESH,
        )

    def out_cols(k):
        b, h, _ = block_at(k)
        return pl.ds(pl.multiple_of((row * n_col + b) * ab_rows + h * CHUNK, CHUNK), CHUNK)

    def r_copy(k, o):
        return pltpu.make_async_remote_copy(
            src_ref=fin.at[k, pl.ds(pl.multiple_of(row_peer(o) * rows_r, rows_r), rows_r)],
            dst_ref=out_ref.at[:, out_cols(k)],
            send_sem=r_send.at[k, o - 1],
            recv_sem=r_recv.at[k, o - 1],
            device_id={"row": row_peer(o)},
            device_id_type=MESH,
        )

    def d_copy(k, o):
        h = k % n_ch
        return pltpu.make_async_remote_copy(
            src_ref=fin.at[k, pl.ds(pl.multiple_of(row_peer(o) * rows_r, rows_r), rows_r)],
            dst_ref=out_ref.at[:, out_cols(k)],
            send_sem=d_send.at[h, o],
            recv_sem=d_recv.at[h, o],
            device_id={"row": row_peer(o), "col": end_col},
            device_id_type=MESH,
        )

    def step(k, c):
        @pl.when(helps & (k == steps - 4))
        def _():
            take(0)

        @pl.when(helps & (k == steps - 3))
        def _():
            take(1)

        @pl.when(helps & (k == steps - 1))
        def _():
            place_own(0)
            place_own(1)
            place_peers(0)
            take(2)
            place_own(2)
            take(3)
            place_own(3)

        @pl.when(helps & (k == steps))
        def _():
            for p in range(1, n_depth):
                place_peers(p)

        @pl.when(k == normal - 3)
        def _():
            near_sends("wait_send", 0)
            near_sends("start", 1)

        @pl.when(at_end & (k == normal - 2))
        def _():
            e_copy(0).wait_send()
            e_copy(1).wait_send()
            e_copy(2).start()
            e_copy(3).start()

        @pl.when(k < total_steps)
        def _():
            b, h, s = block_at(k)
            which = jnp.where(k < steps, 0, 1)

            @pl.when((s >= 2) & (k < steps))
            def _():
                w_copy(wg, b, h, 0).wait_recv()

            w_t = wg[b, pl.ds(pl.multiple_of(h * CHUNK, CHUNK), CHUNK), :].T
            wh, wl = halves(w_t)
            w3 = jnp.concatenate([wh, wh, wl], axis=0)
            tile = rows_all // 2
            for m in range(2):
                at = pl.ds(m * tile, tile)
                a = th[which, at, :]
                a3 = jnp.concatenate([a, tl[which, at, :], a], axis=1)
                part[k, at, :] = jnp.dot(a3, w3, preferred_element_type=jnp.float32)
            s1_copy(k).start()

        @pl.when((k >= 1) & (k < total_steps + 1))
        def _():
            j = k - 1
            s1_copy(j).wait_recv()
            at = pl.ds(pl.multiple_of(lo * rows_lo, rows_lo), rows_lo)
            part[j, at, :] = part[j, at, :] + recv1[j]
            for o in range(1, n_hi):
                s2_copy(j, o).start()

        @pl.when(k >= 2)
        def _():
            j = k - 2
            total = part[j, pl.ds(pl.multiple_of(lo * rows_lo + hi * rows_d, rows_d), rows_d), :]
            for o in range(1, n_hi):
                s2_copy(j, o).wait_recv()
                total = total + recv2[j, o - 1]
            fin[j] = total

            @pl.when(j < normal)
            def _():
                for o in range(1, n_row):
                    r_copy(j, o).start()
                out_ref[:, out_cols(j)] = fin[j, pl.ds(pl.multiple_of(row * rows_r, rows_r), rows_r), :]

            @pl.when(j >= normal)
            def _():
                for o in range(n_row):
                    d_copy(j, o).start()

        return c

    lax.fori_loop(0, total_steps + 2, step, 0)

    def drain(k, c):
        s1_copy(k).wait_send()
        for o in range(1, n_hi):
            s2_copy(k, o).wait_send()

        @pl.when(k < normal)
        def _():
            for o in range(1, n_row):
                r_copy(k, o).wait_send()
                r_copy(k, o).wait_recv()

        @pl.when(k >= normal)
        def _():
            for o in range(n_row):
                d_copy(k, o).wait_send()

        return c

    lax.fori_loop(0, total_steps, drain, 0)

    near_sends("wait_send", 1)

    @pl.when(at_end)
    def _():
        e_copy(2).wait_send()
        e_copy(3).wait_send()
        for h in range(n_ch):
            for o in range(n_row):
                d_copy(h, o).wait_recv()

    if not gathered:

        @pl.when(helps)
        def _():
            for p in range(n_depth):
                for o in range(1, n_row):
                    x_copy(p, o).wait_send()

    if not gathered:
        for o in range(1, n_row):
            t_copy(o).wait_send()


def shards(sizes, integrals, amplitudes):
    n_row, n_col, n_depth = sizes
    n_lo = LANES
    n_hi = n_depth // n_lo
    kc, i_count, j_local = amplitudes.shape
    j_count = j_local * n_row
    ab_rows = integrals.shape[0]
    n_ch = ab_rows // CHUNK
    slots = (n_col + 1) * n_ch
    rows_all = i_count * j_count
    rows_lo = rows_all // n_lo
    rows_d = rows_lo // n_hi
    rows_r = rows_d // n_row
    i_out = i_count // n_depth
    gathered = j_local % (16 * n_row) != 0
    side = i_out * j_local
    tiny = j_local if gathered else n_row
    source = np.arange(side).reshape(i_out, j_local // tiny, tiny).transpose(2, 0, 1).reshape(-1)
    order = jnp.asarray(np.eye(side)[source], jnp.bfloat16)
    t = jnp.transpose(amplitudes, (1, 2, 0))
    if gathered:
        t = lax.all_gather(t, "row", axis=1, tiled=True)
        t = t.reshape(n_hi, n_lo, i_out, j_count // n_row, n_row, kc)
        t = jnp.transpose(t, (1, 0, 4, 2, 3, 5)).reshape(rows_all, kc)
        tg = pltpu.VMEM(t.shape, jnp.float32)
    else:
        tg = pltpu.VMEM((n_row,) + t.shape, jnp.float32)
    dma = pltpu.SemaphoreType.DMA
    out = pl.pallas_call(
        functools.partial(kernel, sizes, gathered),
        out_shape=jax.ShapeDtypeStruct((rows_r, n_row * n_col * ab_rows), jnp.float32),
        in_specs=[pl.BlockSpec(memory_space=pl.ANY)] * 2 + [pl.BlockSpec(memory_space=pltpu.VMEM)],
        out_specs=pl.BlockSpec(memory_space=pltpu.VMEM),
        scratch_shapes=[
            pltpu.VMEM((n_col, ab_rows, kc), jnp.float32),
            tg,
            tg,
            pltpu.VMEM((2, rows_all, kc), jnp.bfloat16),
            pltpu.VMEM((2, rows_all, kc), jnp.bfloat16),
            pltpu.VMEM((slots, rows_all, CHUNK), jnp.float32),
            pltpu.VMEM((slots, rows_lo, CHUNK), jnp.float32),
            pltpu.VMEM((slots, max(n_hi - 1, 1), rows_d, CHUNK), jnp.float32),
            pltpu.VMEM((slots, rows_d, CHUNK), jnp.float32),
            dma((2,)),
            dma((2, n_col, ab_rows // CHUNK)),
            dma((n_col, ab_rows // CHUNK)),
            dma((max(n_row - 1, 1),)),
            dma((max(n_row - 1, 1),)),
            dma((slots,)),
            dma((slots,)),
            dma((slots, max(n_hi - 1, 1))),
            dma((slots, max(n_hi - 1, 1))),
            dma((slots, max(n_row - 1, 1))),
            dma((slots, max(n_row - 1, 1))),
            dma((n_depth,)),
            dma((n_depth,)),
            dma((n_depth, max(n_row - 1, 1))),
            dma((n_depth, max(n_row - 1, 1))),
            dma((n_ch, n_row)),
            dma((n_ch, n_row)),
        ],
        compiler_params=pltpu.CompilerParams(
            collective_id=0, has_side_effects=True, vmem_limit_bytes=60 * 2**20
        ),
        cost_estimate=pl.CostEstimate(
            flops=6 * rows_all * kc * ab_rows * n_col, bytes_accessed=6 * 2**20, transcendentals=0
        ),
    )(integrals, t, order)
    return out.reshape(i_out, j_count // n_row, n_row * n_col * ab_rows)


def solution(mesh):
    sizes = (mesh.shape["row"], mesh.shape["col"], mesh.shape["depth"])
    placed = (P(("row", "col"), "depth"), P("depth", "col", "row"))
    return jax.shard_map(
        functools.partial(shards, sizes),
        mesh=mesh,
        in_specs=placed,
        out_specs=P(("col", "depth"), "row", None),
        check_vma=False,
    )
```

```python
import functools

import jax
import jax.numpy as jnp
import numpy as np
from jax import lax
from jax.experimental import pallas as pl
from jax.experimental.pallas import tpu as pltpu
from jax.sharding import PartitionSpec as P

MESH = pl.DeviceIdType.MESH
CHUNK = 256
LANES = 2


def halves(x):
    hi = x.astype(jnp.bfloat16)
    lo = (x - hi.astype(jnp.float32)).astype(jnp.bfloat16)
    return hi, lo


def kernel(sizes, gathered, w_ref, t_ref, order_ref, out_ref, wg, tg, tg2, th, tl, part, recv1, recv2, fin,
           own_sem, w_send, w_recv, t_send, t_recv, s1_send, s1_recv, s2_send, s2_recv, r_send, r_recv,
           e_send, e_recv, f_send, f_recv, x_send, x_recv, d_send, d_recv):
    n_row, n_col, n_depth = sizes
    n_lo = LANES
    n_hi = n_depth // n_lo
    ab_rows = w_ref.shape[0]
    n_ch = ab_rows // CHUNK
    assert n_ch == 2 and n_depth == 4 and n_col == 4
    steps = n_col * n_ch
    rows_all = th.shape[1]
    rows_lo = rows_all // n_lo
    rows_d = rows_lo // n_hi
    rows_r = rows_d // n_row
    row, col, depth = lax.axis_index("row"), lax.axis_index("col"), lax.axis_index("depth")
    hi, lo = depth // n_lo, depth % n_lo

    def row_peer(o):
        return (row + o) % n_row

    def hi_peer(o):
        return (hi + o) % n_hi

    mate = hi * n_lo + (1 - lo)
    at_end = (col == 0) | (col == n_col - 1)
    helps = (col == 1) | (col == n_col - 2)
    far = jnp.where(col < n_col // 2, n_col - 1, 0)
    end_col = jnp.where(col < n_col // 2, 0, n_col - 1)
    help_col = jnp.where(col < n_col // 2, 1, n_col - 2)
    normal = jnp.where(at_end, steps - n_ch, steps)
    total_steps = jnp.where(helps, steps + n_ch, normal)

    barrier = pltpu.get_barrier_semaphore()
    for o in range(1, n_row):
        pl.semaphore_signal(barrier, inc=1, device_id={"row": row_peer(o)}, device_id_type=MESH)
    pl.semaphore_signal(barrier, inc=1, device_id={"depth": mate}, device_id_type=MESH)
    for o in range(1, n_hi):
        pl.semaphore_signal(barrier, inc=1, device_id={"depth": hi_peer(o) * n_lo + lo}, device_id_type=MESH)

    @pl.when(col > 0)
    def _():
        pl.semaphore_signal(barrier, inc=1, device_id={"col": col - 1}, device_id_type=MESH)

    @pl.when(col < n_col - 1)
    def _():
        pl.semaphore_signal(barrier, inc=1, device_id={"col": col + 1}, device_id_type=MESH)

    for o in range(1, n_row):

        @pl.when(at_end)
        def _():
            pl.semaphore_signal(
                barrier, inc=1, device_id={"row": row_peer(o), "col": help_col}, device_id_type=MESH
            )

        @pl.when(helps)
        def _():
            pl.semaphore_signal(
                barrier, inc=1, device_id={"row": row_peer(o), "col": end_col}, device_id_type=MESH
            )

    fixed = (n_row - 1) + 1 + (n_hi - 1)
    ends = jnp.where(col > 0, 1, 0) + jnp.where(col < n_col - 1, 1, 0)
    diagonal = jnp.where(at_end | helps, n_row - 1, 0)
    pl.semaphore_wait(barrier, fixed + ends + diagonal)

    def w_copy(src, b, h, side):
        rows = pl.ds(pl.multiple_of(h * CHUNK, CHUNK), CHUNK)
        to = jnp.clip(col + (1 if side else -1), 0, n_col - 1)
        return pltpu.make_async_remote_copy(
            src_ref=w_ref.at[rows] if src is None else wg.at[b, rows],
            dst_ref=wg.at[b, rows],
            send_sem=w_send.at[side, b, h],
            recv_sem=w_recv.at[b, h],
            device_id={"col": to},
            device_id_type=MESH,
        )

    def own_sends(act, h):
        @pl.when(col > 0)
        def _():
            getattr(w_copy(None, col, h, 0), act)()

        @pl.when(col < n_col - 1)
        def _():
            getattr(w_copy(None, col, h, 1), act)()

    def near_sends(act, h):
        @pl.when((col > 0) & goes_right(col - 1))
        def _():
            getattr(w_copy(wg, col - 1, h, 1), act)()

        @pl.when((col < n_col - 1) & goes_left(col + 1))
        def _():
            getattr(w_copy(wg, col + 1, h, 0), act)()

    def near_arrive(h):
        @pl.when(col > 0)
        def _():
            w_copy(wg, col - 1, h, 0).wait_recv()

        @pl.when(col < n_col - 1)
        def _():
            w_copy(wg, col + 1, h, 0).wait_recv()

    def goes_right(b):
        return (col < n_col - 1) & ((b > 0) | (col < n_col - 2))

    def goes_left(b):
        return (col > 0) & ((b < n_col - 1) | (col > 1))

    own_sends("start", 0)

    def t_copy(o):
        return pltpu.make_async_remote_copy(
            src_ref=t_ref,
            dst_ref=tg.at[row],
            send_sem=t_send.at[o - 1],
            recv_sem=t_recv.at[o - 1],
            device_id={"row": row_peer(o)},
            device_id_type=MESH,
        )

    if not gathered:
        for o in range(1, n_row):
            t_copy(o).start()
        t_own = pltpu.make_async_copy(t_ref, tg.at[row], own_sem.at[1])
    else:
        t_own = pltpu.make_async_copy(t_ref, tg, own_sem.at[1])
    t_own.start()
    w_own = pltpu.make_async_copy(w_ref, wg.at[col], own_sem.at[0])
    w_own.start()

    def place(src, which, q, first, last):
        i_count, j_local, kc = t_ref.shape
        i_out = i_count // n_depth
        per_r = j_local // n_row
        order = order_ref[...]

        def body(d, c):
            x = src[q, pl.ds(d * i_out, i_out)].reshape(i_out * j_local, kc)
            base = (d % n_lo) * rows_lo + (d // n_lo) * rows_d
            for x_part, into in zip(halves(x), (th, tl)):
                y = jnp.dot(order, x_part, preferred_element_type=jnp.float32).astype(jnp.bfloat16)
                for piece in range(n_row * i_out):
                    at = base + piece * (per_r * n_row) + q * per_r
                    into[which, pl.ds(pl.multiple_of(at, per_r), per_r), :] = y[piece * per_r : (piece + 1) * per_r]
            return c

        lax.fori_loop(first, last, body, 0)

    def plain(src, which, first, last):
        def body(m, c):
            at = pl.ds(pl.multiple_of(m * 64, 64), 64)
            th[which, at, :], tl[which, at, :] = halves(src[at, :])
            return c

        lax.fori_loop(first * (rows_all // 64) // n_depth, last * (rows_all // 64) // n_depth, body, 0)

    piece = t_ref.shape[0] // n_depth
    n_swap = n_depth // 2

    def e_copy(p):
        rows = pl.ds(p * piece, piece)
        return pltpu.make_async_remote_copy(
            src_ref=t_ref.at[rows],
            dst_ref=tg2.at[rows] if gathered else tg2.at[row, rows],
            send_sem=e_send.at[p],
            recv_sem=e_recv.at[p],
            device_id={"col": help_col},
            device_id_type=MESH,
        )

    def x_copy(p, o):
        rows = pl.ds(p * piece, piece)
        return pltpu.make_async_remote_copy(
            src_ref=tg2.at[row, rows],
            dst_ref=tg2.at[row, rows],
            send_sem=x_send.at[p, o - 1],
            recv_sem=x_recv.at[p, o - 1],
            device_id={"row": row_peer(o)},
            device_id_type=MESH,
        )

    def f_copy(p, o):
        q = (row + n_row - o) % n_row
        rows = pl.ds(p * piece, piece)
        return pltpu.make_async_remote_copy(
            src_ref=tg.at[q, rows],
            dst_ref=tg2.at[q, rows],
            send_sem=f_send.at[p, o - 1],
            recv_sem=f_recv.at[p, o - 1],
            device_id={"col": help_col},
            device_id_type=MESH,
        )

    def take(p):
        e_copy(p).wait_recv()
        if not gathered and p < n_swap:
            for o in range(1, n_row):
                x_copy(p, o).start()

    def place_own(p):
        if gathered:
            plain(tg2, 1, p, p + 1)
        else:
            place(tg2, 1, row, p, p + 1)

    def place_peers(p):
        if not gathered:
            for o in range(1, n_row):
                (x_copy if p < n_swap else f_copy)(p, o).wait_recv()
                place(tg2, 1, (row + n_row - o) % n_row, p, p + 1)

    t_own.wait()
    if not gathered:
        place(tg, 0, row, 0, n_depth)
    else:
        plain(tg, 0, 0, n_depth)

    own_sends("wait_send", 0)
    own_sends("start", 1)
    near_arrive(0)
    own_sends("wait_send", 1)
    near_sends("start", 0)

    @pl.when(at_end)
    def _():
        e_copy(0).start()
        e_copy(1).start()

    near_arrive(1)
    if not gathered:
        for o in range(1, n_row):
            t_copy(o).wait_recv()
            place(tg, 0, (row + n_row - o) % n_row, 0, n_depth)
    w_own.wait()

    near = jnp.minimum(col, n_col - 1 - col)

    def block_at(k):
        p, h = k // n_ch, k % n_ch
        both = p <= 2 * near
        s = jnp.where(both, (p + 1) // 2, p - near)
        left = jnp.where(both, p % 2 == 1, col > near)
        b = jnp.where(p == 0, col, jnp.where(left, col - s, col + s))
        return jnp.where(p < n_col, b, far), h, s

    def s1_copy(k):
        return pltpu.make_async_remote_copy(
            src_ref=part.at[k, pl.ds(pl.multiple_of((1 - lo) * rows_lo, rows_lo), rows_lo)],
            dst_ref=recv1.at[k],
            send_sem=s1_send.at[k],
            recv_sem=s1_recv.at[k],
            device_id={"depth": mate},
            device_id_type=MESH,
        )

    def s2_copy(k, o):
        return pltpu.make_async_remote_copy(
            src_ref=part.at[k, pl.ds(pl.multiple_of(lo * rows_lo + hi_peer(o) * rows_d, rows_d), rows_d)],
            dst_ref=recv2.at[k, o - 1],
            send_sem=s2_send.at[k, o - 1],
            recv_sem=s2_recv.at[k, o - 1],
            device_id={"depth": hi_peer(o) * n_lo + lo},
            device_id_type=MESH,
        )

    def out_cols(k):
        b, h, _ = block_at(k)
        return pl.ds(pl.multiple_of((row * n_col + b) * ab_rows + h * CHUNK, CHUNK), CHUNK)

    def r_copy(k, o):
        return pltpu.make_async_remote_copy(
            src_ref=fin.at[k, pl.ds(pl.multiple_of(row_peer(o) * rows_r, rows_r), rows_r)],
            dst_ref=out_ref.at[:, out_cols(k)],
            send_sem=r_send.at[k, o - 1],
            recv_sem=r_recv.at[k, o - 1],
            device_id={"row": row_peer(o)},
            device_id_type=MESH,
        )

    def d_copy(k, o):
        h = k % n_ch
        return pltpu.make_async_remote_copy(
            src_ref=fin.at[k, pl.ds(pl.multiple_of(row_peer(o) * rows_r, rows_r), rows_r)],
            dst_ref=out_ref.at[:, out_cols(k)],
            send_sem=d_send.at[h, o],
            recv_sem=d_recv.at[h, o],
            device_id={"row": row_peer(o), "col": end_col},
            device_id_type=MESH,
        )

    def step(k, c):
        @pl.when(helps & (k == steps - 4))
        def _():
            take(0)

        @pl.when(helps & (k == steps - 3))
        def _():
            take(1)

        @pl.when(helps & (k == steps - 1))
        def _():
            place_own(0)
            place_own(1)
            place_peers(0)

        @pl.when(helps & (k == steps))
        def _():
            place_peers(1)
            for p in range(n_swap, n_depth):
                take(p)
                place_own(p)
                place_peers(p)

        @pl.when(k == normal - 3)
        def _():
            near_sends("wait_send", 0)
            near_sends("start", 1)

        @pl.when(at_end & (k == normal - 3))
        def _():
            for p in range(n_swap):
                e_copy(p).wait_send()
            for p in range(n_swap, n_depth):
                e_copy(p).start()
                if not gathered:
                    for o in range(1, n_row):
                        f_copy(p, o).start()

        @pl.when(k < total_steps)
        def _():
            b, h, s = block_at(k)
            which = jnp.where(k < steps, 0, 1)

            @pl.when((s >= 2) & (k < steps))
            def _():
                w_copy(wg, b, h, 0).wait_recv()

            w_t = wg[b, pl.ds(pl.multiple_of(h * CHUNK, CHUNK), CHUNK), :].T
            wh, wl = halves(w_t)
            w3 = jnp.concatenate([wh, wh, wl], axis=0)
            tile = rows_all // 2
            for m in range(2):
                at = pl.ds(m * tile, tile)
                a = th[which, at, :]
                a3 = jnp.concatenate([a, tl[which, at, :], a], axis=1)
                part[k, at, :] = jnp.dot(a3, w3, preferred_element_type=jnp.float32)
            s1_copy(k).start()

        @pl.when((k >= 1) & (k < total_steps + 1))
        def _():
            j = k - 1
            s1_copy(j).wait_recv()
            at = pl.ds(pl.multiple_of(lo * rows_lo, rows_lo), rows_lo)
            part[j, at, :] = part[j, at, :] + recv1[j]
            for o in range(1, n_hi):
                s2_copy(j, o).start()

        @pl.when(k >= 2)
        def _():
            j = k - 2
            total = part[j, pl.ds(pl.multiple_of(lo * rows_lo + hi * rows_d, rows_d), rows_d), :]
            for o in range(1, n_hi):
                s2_copy(j, o).wait_recv()
                total = total + recv2[j, o - 1]
            fin[j] = total

            @pl.when(j < normal)
            def _():
                for o in range(1, n_row):
                    r_copy(j, o).start()
                out_ref[:, out_cols(j)] = fin[j, pl.ds(pl.multiple_of(row * rows_r, rows_r), rows_r), :]

            @pl.when(j >= normal)
            def _():
                for o in range(n_row):
                    d_copy(j, o).start()

        return c

    lax.fori_loop(0, total_steps + 2, step, 0)

    def drain(k, c):
        s1_copy(k).wait_send()
        for o in range(1, n_hi):
            s2_copy(k, o).wait_send()

        @pl.when(k < normal)
        def _():
            for o in range(1, n_row):
                r_copy(k, o).wait_send()
                r_copy(k, o).wait_recv()

        @pl.when(k >= normal)
        def _():
            for o in range(n_row):
                d_copy(k, o).wait_send()

        return c

    lax.fori_loop(0, total_steps, drain, 0)

    near_sends("wait_send", 1)

    @pl.when(at_end)
    def _():
        for p in range(n_swap, n_depth):
            e_copy(p).wait_send()
            if not gathered:
                for o in range(1, n_row):
                    f_copy(p, o).wait_send()
        for h in range(n_ch):
            for o in range(n_row):
                d_copy(h, o).wait_recv()

    if not gathered:

        @pl.when(helps)
        def _():
            for p in range(n_swap):
                for o in range(1, n_row):
                    x_copy(p, o).wait_send()

    if not gathered:
        for o in range(1, n_row):
            t_copy(o).wait_send()


def shards(sizes, integrals, amplitudes):
    n_row, n_col, n_depth = sizes
    n_lo = LANES
    n_hi = n_depth // n_lo
    kc, i_count, j_local = amplitudes.shape
    j_count = j_local * n_row
    ab_rows = integrals.shape[0]
    n_ch = ab_rows // CHUNK
    slots = (n_col + 1) * n_ch
    rows_all = i_count * j_count
    rows_lo = rows_all // n_lo
    rows_d = rows_lo // n_hi
    rows_r = rows_d // n_row
    i_out = i_count // n_depth
    gathered = j_local % (16 * n_row) != 0
    side = i_out * j_local
    tiny = j_local if gathered else n_row
    source = np.arange(side).reshape(i_out, j_local // tiny, tiny).transpose(2, 0, 1).reshape(-1)
    order = jnp.asarray(np.eye(side)[source], jnp.bfloat16)
    t = jnp.transpose(amplitudes, (1, 2, 0))
    if gathered:
        t = lax.all_gather(t, "row", axis=1, tiled=True)
        t = t.reshape(n_hi, n_lo, i_out, j_count // n_row, n_row, kc)
        t = jnp.transpose(t, (1, 0, 4, 2, 3, 5)).reshape(rows_all, kc)
        tg = pltpu.VMEM(t.shape, jnp.float32)
    else:
        tg = pltpu.VMEM((n_row,) + t.shape, jnp.float32)
    dma = pltpu.SemaphoreType.DMA
    out = pl.pallas_call(
        functools.partial(kernel, sizes, gathered),
        out_shape=jax.ShapeDtypeStruct((rows_r, n_row * n_col * ab_rows), jnp.float32),
        in_specs=[pl.BlockSpec(memory_space=pl.ANY)] * 2 + [pl.BlockSpec(memory_space=pltpu.VMEM)],
        out_specs=pl.BlockSpec(memory_space=pltpu.VMEM),
        scratch_shapes=[
            pltpu.VMEM((n_col, ab_rows, kc), jnp.float32),
            tg,
            tg,
            pltpu.VMEM((2, rows_all, kc), jnp.bfloat16),
            pltpu.VMEM((2, rows_all, kc), jnp.bfloat16),
            pltpu.VMEM((slots, rows_all, CHUNK), jnp.float32),
            pltpu.VMEM((slots, rows_lo, CHUNK), jnp.float32),
            pltpu.VMEM((slots, max(n_hi - 1, 1), rows_d, CHUNK), jnp.float32),
            pltpu.VMEM((slots, rows_d, CHUNK), jnp.float32),
            dma((2,)),
            dma((2, n_col, ab_rows // CHUNK)),
            dma((n_col, ab_rows // CHUNK)),
            dma((max(n_row - 1, 1),)),
            dma((max(n_row - 1, 1),)),
            dma((slots,)),
            dma((slots,)),
            dma((slots, max(n_hi - 1, 1))),
            dma((slots, max(n_hi - 1, 1))),
            dma((slots, max(n_row - 1, 1))),
            dma((slots, max(n_row - 1, 1))),
            dma((n_depth,)),
            dma((n_depth,)),
            dma((n_depth, max(n_row - 1, 1))),
            dma((n_depth, max(n_row - 1, 1))),
            dma((n_depth, max(n_row - 1, 1))),
            dma((n_depth, max(n_row - 1, 1))),
            dma((n_ch, n_row)),
            dma((n_ch, n_row)),
        ],
        compiler_params=pltpu.CompilerParams(
            collective_id=0, has_side_effects=True, vmem_limit_bytes=60 * 2**20
        ),
        cost_estimate=pl.CostEstimate(
            flops=6 * rows_all * kc * ab_rows * n_col, bytes_accessed=6 * 2**20, transcendentals=0
        ),
    )(integrals, t, order)
    return out.reshape(i_out, j_count // n_row, n_row * n_col * ab_rows)


def solution(mesh):
    sizes = (mesh.shape["row"], mesh.shape["col"], mesh.shape["depth"])
    placed = (P(("row", "col"), "depth"), P("depth", "col", "row"))
    return jax.shard_map(
        functools.partial(shards, sizes),
        mesh=mesh,
        in_specs=placed,
        out_specs=P(("col", "depth"), "row", None),
        check_vma=False,
    )
```

```python
import functools

import jax
import jax.numpy as jnp
import numpy as np
from jax import lax
from jax.experimental import pallas as pl
from jax.experimental.pallas import tpu as pltpu
from jax.sharding import PartitionSpec as P

MESH = pl.DeviceIdType.MESH
CHUNK = 256
LANES = 2


def halves(x):
    hi = x.astype(jnp.bfloat16)
    lo = (x - hi.astype(jnp.float32)).astype(jnp.bfloat16)
    return hi, lo


def kernel(sizes, gathered, w_ref, t_ref, order_ref, out_ref, wg, tg, tg2, th, tl, part, recv1, recv2, fin,
           part_d, recv1_d, recv2_d, fin_d,
           own_sem, w_send, w_recv, t_send, t_recv, s1_send, s1_recv, s2_send, s2_recv, r_send, r_recv,
           e_send, e_recv, f_send, f_recv, x_send, x_recv, d1_send, d1_recv, d2_send, d2_recv, d_send, d_recv):
    n_row, n_col, n_depth = sizes
    n_lo = LANES
    n_hi = n_depth // n_lo
    ab_rows = w_ref.shape[0]
    n_ch = ab_rows // CHUNK
    assert n_ch == 2 and n_depth == 4 and n_col == 4
    steps = n_col * n_ch
    rows_all = th.shape[1]
    rows_lo = rows_all // n_lo
    rows_d = rows_lo // n_hi
    rows_r = rows_d // n_row
    row, col, depth = lax.axis_index("row"), lax.axis_index("col"), lax.axis_index("depth")
    hi, lo = depth // n_lo, depth % n_lo

    def row_peer(o):
        return (row + o) % n_row

    def hi_peer(o):
        return (hi + o) % n_hi

    mate = hi * n_lo + (1 - lo)
    at_end = (col == 0) | (col == n_col - 1)
    helps = (col == 1) | (col == n_col - 2)
    far = jnp.where(col < n_col // 2, n_col - 1, 0)
    end_col = jnp.where(col < n_col // 2, 0, n_col - 1)
    help_col = jnp.where(col < n_col // 2, 1, n_col - 2)
    normal = jnp.where(at_end, steps - n_ch, steps)

    barrier = pltpu.get_barrier_semaphore()
    for o in range(1, n_row):
        pl.semaphore_signal(barrier, inc=1, device_id={"row": row_peer(o)}, device_id_type=MESH)
    pl.semaphore_signal(barrier, inc=1, device_id={"depth": mate}, device_id_type=MESH)
    for o in range(1, n_hi):
        pl.semaphore_signal(barrier, inc=1, device_id={"depth": hi_peer(o) * n_lo + lo}, device_id_type=MESH)

    @pl.when(col > 0)
    def _():
        pl.semaphore_signal(barrier, inc=1, device_id={"col": col - 1}, device_id_type=MESH)

    @pl.when(col < n_col - 1)
    def _():
        pl.semaphore_signal(barrier, inc=1, device_id={"col": col + 1}, device_id_type=MESH)

    for o in range(1, n_row):

        @pl.when(at_end)
        def _():
            pl.semaphore_signal(
                barrier, inc=1, device_id={"row": row_peer(o), "col": help_col}, device_id_type=MESH
            )

        @pl.when(helps)
        def _():
            pl.semaphore_signal(
                barrier, inc=1, device_id={"row": row_peer(o), "col": end_col}, device_id_type=MESH
            )

    fixed = (n_row - 1) + 1 + (n_hi - 1)
    ends = jnp.where(col > 0, 1, 0) + jnp.where(col < n_col - 1, 1, 0)
    diagonal = jnp.where(at_end | helps, n_row - 1, 0)
    pl.semaphore_wait(barrier, fixed + ends + diagonal)

    def w_copy(src, b, h, side):
        rows = pl.ds(pl.multiple_of(h * CHUNK, CHUNK), CHUNK)
        to = jnp.clip(col + (1 if side else -1), 0, n_col - 1)
        return pltpu.make_async_remote_copy(
            src_ref=w_ref.at[rows] if src is None else wg.at[b, rows],
            dst_ref=wg.at[b, rows],
            send_sem=w_send.at[side, b, h],
            recv_sem=w_recv.at[b, h],
            device_id={"col": to},
            device_id_type=MESH,
        )

    def own_sends(act, h):
        @pl.when(col > 0)
        def _():
            getattr(w_copy(None, col, h, 0), act)()

        @pl.when(col < n_col - 1)
        def _():
            getattr(w_copy(None, col, h, 1), act)()

    def near_sends(act, h):
        @pl.when((col > 0) & goes_right(col - 1))
        def _():
            getattr(w_copy(wg, col - 1, h, 1), act)()

        @pl.when((col < n_col - 1) & goes_left(col + 1))
        def _():
            getattr(w_copy(wg, col + 1, h, 0), act)()

    def near_arrive(h):
        @pl.when(col > 0)
        def _():
            w_copy(wg, col - 1, h, 0).wait_recv()

        @pl.when(col < n_col - 1)
        def _():
            w_copy(wg, col + 1, h, 0).wait_recv()

    def goes_right(b):
        return (col < n_col - 1) & ((b > 0) | (col < n_col - 2))

    def goes_left(b):
        return (col > 0) & ((b < n_col - 1) | (col > 1))

    own_sends("start", 0)

    def t_copy(o):
        return pltpu.make_async_remote_copy(
            src_ref=t_ref,
            dst_ref=tg.at[row],
            send_sem=t_send.at[o - 1],
            recv_sem=t_recv.at[o - 1],
            device_id={"row": row_peer(o)},
            device_id_type=MESH,
        )

    if not gathered:
        for o in range(1, n_row):
            t_copy(o).start()
        t_own = pltpu.make_async_copy(t_ref, tg.at[row], own_sem.at[1])
    else:
        t_own = pltpu.make_async_copy(t_ref, tg, own_sem.at[1])
    t_own.start()
    w_own = pltpu.make_async_copy(w_ref, wg.at[col], own_sem.at[0])
    w_own.start()

    def place(src, q):
        i_out, j_local, kc = t_ref.shape[1:]
        per_r = j_local // n_row
        order = order_ref[...]

        def body(d, c):
            x = src[q, d].reshape(i_out * j_local, kc)
            base = (d % n_lo) * rows_lo + (d // n_lo) * rows_d
            for x_part, into in zip(halves(x), (th, tl)):
                y = jnp.dot(order, x_part, preferred_element_type=jnp.float32).astype(jnp.bfloat16)
                for n in range(n_row * i_out):
                    at = base + n * (per_r * n_row) + q * per_r
                    into[0, pl.ds(pl.multiple_of(at, per_r), per_r), :] = y[n * per_r : (n + 1) * per_r]
            return c

        lax.fori_loop(0, n_depth, body, 0)

    def place_piece(q, p):
        i_out, j_local, kc = t_ref.shape[1:]
        per_r = j_local // n_row
        x = tg2[q, :, p].reshape(n_depth * j_local, kc)
        for x_part, into in zip(halves(x), (th, tl)):
            y = jnp.dot(order_ref[...], x_part, preferred_element_type=jnp.float32).astype(jnp.bfloat16)
            for n in range(n_row * n_depth):
                r, d = n // n_depth, n % n_depth
                base = (p // 2) * rows_all + (d % n_lo) * rows_lo + (d // n_lo) * rows_d + r * rows_r
                at = base // 2 + (p % 2) * (per_r * n_row) + q * per_r
                into[1, pl.ds(pl.multiple_of(at, per_r), per_r), :] = y[n * per_r : (n + 1) * per_r]

    def plain_groups():
        for d in range(n_depth):
            base = (d % n_lo) * rows_lo + (d // n_lo) * rows_d
            x = tg2[pl.ds(base, rows_d), :].reshape(n_row, 2, rows_r // 2, -1)
            for g in range(2):
                at = pl.ds((g * rows_all + base) // 2, rows_d // 2)
                th[1, at, :], tl[1, at, :] = halves(x[:, g].reshape(rows_d // 2, -1))

    def plain():
        def body(m, c):
            at = pl.ds(pl.multiple_of(m * 64, 64), 64)
            th[0, at, :], tl[0, at, :] = halves(tg[at, :])
            return c

        lax.fori_loop(0, rows_all // 64, body, 0)

    piece = rows_all // n_depth
    n_swap = n_depth // 2

    def e_copy(p):
        rows = pl.ds(p * piece, piece)
        return pltpu.make_async_remote_copy(
            src_ref=t_ref.at[rows] if gathered else t_ref.at[:, p],
            dst_ref=tg2.at[rows] if gathered else tg2.at[row, :, p],
            send_sem=e_send.at[p],
            recv_sem=e_recv.at[p],
            device_id={"col": help_col},
            device_id_type=MESH,
        )

    def x_copy(p, o):
        return pltpu.make_async_remote_copy(
            src_ref=tg2.at[row, :, p],
            dst_ref=tg2.at[row, :, p],
            send_sem=x_send.at[p, o - 1],
            recv_sem=x_recv.at[p, o - 1],
            device_id={"row": row_peer(o)},
            device_id_type=MESH,
        )

    def f_copy(p, o):
        q = (row + n_row - o) % n_row
        return pltpu.make_async_remote_copy(
            src_ref=tg.at[q, :, p],
            dst_ref=tg2.at[q, :, p],
            send_sem=f_send.at[p, o - 1],
            recv_sem=f_recv.at[p, o - 1],
            device_id={"col": help_col},
            device_id_type=MESH,
        )

    def take(p):
        e_copy(p).wait_recv()
        if not gathered and p < n_swap:
            for o in range(1, n_row):
                x_copy(p, o).start()

    def place_own(p):
        if not gathered:
            place_piece(row, p)

    def place_peers(p):
        if not gathered:
            for o in range(1, n_row):
                (x_copy if p < n_swap else f_copy)(p, o).wait_recv()
                place_piece((row + n_row - o) % n_row, p)

    t_own.wait()
    if not gathered:
        place(tg, row)
    else:
        plain()

    own_sends("wait_send", 0)
    own_sends("start", 1)
    near_arrive(0)
    own_sends("wait_send", 1)
    near_sends("start", 0)

    @pl.when(at_end)
    def _():
        e_copy(0).start()
        e_copy(1).start()

    near_arrive(1)
    if not gathered:
        for o in range(1, n_row):
            t_copy(o).wait_recv()
            place(tg, (row + n_row - o) % n_row)
    w_own.wait()

    near = jnp.minimum(col, n_col - 1 - col)

    def block_at(k):
        p, h = k // n_ch, k % n_ch
        both = p <= 2 * near
        s = jnp.where(both, (p + 1) // 2, p - near)
        left = jnp.where(both, p % 2 == 1, col > near)
        b = jnp.where(p == 0, col, jnp.where(left, col - s, col + s))
        return b, h, s

    def s1_copy(k):
        return pltpu.make_async_remote_copy(
            src_ref=part.at[k, pl.ds(pl.multiple_of((1 - lo) * rows_lo, rows_lo), rows_lo)],
            dst_ref=recv1.at[k],
            send_sem=s1_send.at[k],
            recv_sem=s1_recv.at[k],
            device_id={"depth": mate},
            device_id_type=MESH,
        )

    def s2_copy(k, o):
        return pltpu.make_async_remote_copy(
            src_ref=part.at[k, pl.ds(pl.multiple_of(lo * rows_lo + hi_peer(o) * rows_d, rows_d), rows_d)],
            dst_ref=recv2.at[k, o - 1],
            send_sem=s2_send.at[k, o - 1],
            recv_sem=s2_recv.at[k, o - 1],
            device_id={"depth": hi_peer(o) * n_lo + lo},
            device_id_type=MESH,
        )

    def out_cols(b, h):
        return pl.ds(pl.multiple_of((row * n_col + b) * ab_rows + h * CHUNK, CHUNK), CHUNK)

    def r_copy(k, o):
        return pltpu.make_async_remote_copy(
            src_ref=fin.at[k, pl.ds(pl.multiple_of(row_peer(o) * rows_r, rows_r), rows_r)],
            dst_ref=out_ref.at[:, out_cols(*block_at(k)[:2])],
            send_sem=r_send.at[k, o - 1],
            recv_sem=r_recv.at[k, o - 1],
            device_id={"row": row_peer(o)},
            device_id_type=MESH,
        )

    def d1_copy(n):
        return pltpu.make_async_remote_copy(
            src_ref=part_d.at[n, pl.ds(pl.multiple_of((1 - lo) * (rows_lo // 2), rows_lo // 2), rows_lo // 2)],
            dst_ref=recv1_d.at[n],
            send_sem=d1_send.at[n],
            recv_sem=d1_recv.at[n],
            device_id={"depth": mate},
            device_id_type=MESH,
        )

    def d2_copy(n, o):
        start = lo * (rows_lo // 2) + hi_peer(o) * (rows_d // 2)
        return pltpu.make_async_remote_copy(
            src_ref=part_d.at[n, pl.ds(pl.multiple_of(start, rows_d // 2), rows_d // 2)],
            dst_ref=recv2_d.at[n, o - 1],
            send_sem=d2_send.at[n, o - 1],
            recv_sem=d2_recv.at[n, o - 1],
            device_id={"depth": hi_peer(o) * n_lo + lo},
            device_id_type=MESH,
        )

    def d_copy(n, o):
        g, h = n // n_ch, n % n_ch
        half = rows_r // 2
        return pltpu.make_async_remote_copy(
            src_ref=fin_d.at[n, pl.ds(pl.multiple_of(row_peer(o) * half, half), half)],
            dst_ref=out_ref.at[pl.ds(g * half, half), out_cols(far, h)],
            send_sem=d_send.at[n, o],
            recv_sem=d_recv.at[n, o],
            device_id={"row": row_peer(o), "col": end_col},
            device_id_type=MESH,
        )

    def multiply(b, h, which, first, tile):
        w_t = wg[b, pl.ds(pl.multiple_of(h * CHUNK, CHUNK), CHUNK), :].T
        wh, wl = halves(w_t)
        w3 = jnp.concatenate([wh, wh, wl], axis=0)
        for start in first:
            at = pl.ds(start, tile)
            a = th[which, at, :]
            a3 = jnp.concatenate([a, tl[which, at, :], a], axis=1)
            yield start, jnp.dot(a3, w3, preferred_element_type=jnp.float32)

    def d_multiply(n):
        for _, y in multiply(far, n % n_ch, 1, (n // n_ch * (rows_all // 2),), rows_all // 2):
            part_d[n] = y
        d1_copy(n).start()

    def d_pair(n):
        d1_copy(n).wait_recv()
        at = pl.ds(pl.multiple_of(lo * (rows_lo // 2), rows_lo // 2), rows_lo // 2)
        part_d[n, at, :] = part_d[n, at, :] + recv1_d[n]
        for o in range(1, n_hi):
            d2_copy(n, o).start()

    def d_finish(n):
        start = lo * (rows_lo // 2) + hi * (rows_d // 2)
        total = part_d[n, pl.ds(pl.multiple_of(start, rows_d // 2), rows_d // 2), :]
        for o in range(1, n_hi):
            d2_copy(n, o).wait_recv()
            total = total + recv2_d[n, o - 1]
        fin_d[n] = total
        for o in range(n_row):
            d_copy(n, o).start()

    def pair(j):
        s1_copy(j).wait_recv()
        at = pl.ds(pl.multiple_of(lo * rows_lo, rows_lo), rows_lo)
        part[j, at, :] = part[j, at, :] + recv1[j]
        for o in range(1, n_hi):
            s2_copy(j, o).start()

    def finish(j):
        total = part[j, pl.ds(pl.multiple_of(lo * rows_lo + hi * rows_d, rows_d), rows_d), :]
        for o in range(1, n_hi):
            s2_copy(j, o).wait_recv()
            total = total + recv2[j, o - 1]
        fin[j] = total
        for o in range(1, n_row):
            r_copy(j, o).start()
        mine = fin[j, pl.ds(pl.multiple_of(row * rows_r, rows_r), rows_r), :]
        out_ref[:, out_cols(*block_at(j)[:2])] = mine

    def step(k, c):
        @pl.when(helps & (k == steps - 4))
        def _():
            take(0)

        @pl.when(helps & (k == steps - 3))
        def _():
            take(1)

        @pl.when(helps & (k == steps - 1))
        def _():
            place_own(0)
            place_own(1)
            place_peers(0)

        @pl.when(k == normal - 3)
        def _():
            near_sends("wait_send", 0)
            near_sends("start", 1)

        @pl.when(at_end & (k == normal - 3))
        def _():
            for p in range(n_swap):
                e_copy(p).wait_send()
            for p in range(n_swap, n_depth):
                e_copy(p).start()
                if not gathered:
                    for o in range(1, n_row):
                        f_copy(p, o).start()

        b, h, s = block_at(k)

        @pl.when(s >= 2)
        def _():
            w_copy(wg, b, h, 0).wait_recv()

        for start, y in multiply(b, h, 0, (0, rows_all // 2), rows_all // 2):
            part[k, pl.ds(start, rows_all // 2), :] = y
        s1_copy(k).start()

        @pl.when(k >= 1)
        def _():
            pair(k - 1)

        @pl.when(k >= 2)
        def _():
            finish(k - 2)

        return c

    lax.fori_loop(0, normal, step, 0)

    @pl.when(helps)
    def _():
        place_peers(1)
        if gathered:
            for p in range(n_swap, n_depth):
                take(p)
            plain_groups()
        d_multiply(0)

    pair(normal - 1)
    finish(normal - 2)

    @pl.when(helps)
    def _():
        d_multiply(1)
        d_pair(0)

    finish(normal - 1)

    @pl.when(helps)
    def _():
        d_pair(1)
        d_finish(0)
        d_finish(1)
        for p in range(n_swap, n_depth):
            if not gathered:
                take(p)
            place_own(p)
            place_peers(p)
        d_multiply(2)
        d_multiply(3)
        d_pair(2)
        d_pair(3)
        d_finish(2)
        d_finish(3)

    def drain(k, c):
        s1_copy(k).wait_send()
        for o in range(1, n_hi):
            s2_copy(k, o).wait_send()
        for o in range(1, n_row):
            r_copy(k, o).wait_send()
            r_copy(k, o).wait_recv()
        return c

    lax.fori_loop(0, normal, drain, 0)

    @pl.when(helps)
    def _():
        for n in range(2 * n_ch):
            d1_copy(n).wait_send()
            for o in range(1, n_hi):
                d2_copy(n, o).wait_send()
            for o in range(n_row):
                d_copy(n, o).wait_send()

    near_sends("wait_send", 1)

    @pl.when(at_end)
    def _():
        for p in range(n_swap, n_depth):
            e_copy(p).wait_send()
            if not gathered:
                for o in range(1, n_row):
                    f_copy(p, o).wait_send()
        for n in range(2 * n_ch):
            for o in range(n_row):
                d_copy(n, o).wait_recv()

    if not gathered:

        @pl.when(helps)
        def _():
            for p in range(n_swap):
                for o in range(1, n_row):
                    x_copy(p, o).wait_send()

    if not gathered:
        for o in range(1, n_row):
            t_copy(o).wait_send()


def shards(sizes, integrals, amplitudes):
    n_row, n_col, n_depth = sizes
    n_lo = LANES
    n_hi = n_depth // n_lo
    kc, i_count, j_local = amplitudes.shape
    j_count = j_local * n_row
    ab_rows = integrals.shape[0]
    n_ch = ab_rows // CHUNK
    slots = n_col * n_ch
    late = 2 * n_ch
    rows_all = i_count * j_count
    rows_lo = rows_all // n_lo
    rows_d = rows_lo // n_hi
    rows_r = rows_d // n_row
    i_out = i_count // n_depth
    gathered = j_local % (16 * n_row) != 0
    side = i_out * j_local
    tiny = j_local if gathered else n_row
    source = np.arange(side).reshape(i_out, j_local // tiny, tiny).transpose(2, 0, 1).reshape(-1)
    order = jnp.asarray(np.eye(side)[source], jnp.bfloat16)
    assert i_out == n_depth
    t = jnp.transpose(amplitudes, (1, 2, 0))
    if gathered:
        t = lax.all_gather(t, "row", axis=1, tiled=True)
        t = t.reshape(n_hi, n_lo, i_out, j_count // n_row, n_row, kc)
        t = jnp.transpose(t, (1, 0, 4, 2, 3, 5)).reshape(rows_all, kc)
        tg = pltpu.VMEM(t.shape, jnp.float32)
    else:
        t = t.reshape(n_depth, i_out, j_local, kc)
        tg = pltpu.VMEM((n_row,) + t.shape, jnp.float32)
    dma = pltpu.SemaphoreType.DMA
    out = pl.pallas_call(
        functools.partial(kernel, sizes, gathered),
        out_shape=jax.ShapeDtypeStruct((rows_r, n_row * n_col * ab_rows), jnp.float32),
        in_specs=[pl.BlockSpec(memory_space=pl.ANY)] * 2 + [pl.BlockSpec(memory_space=pltpu.VMEM)],
        out_specs=pl.BlockSpec(memory_space=pltpu.VMEM),
        scratch_shapes=[
            pltpu.VMEM((n_col, ab_rows, kc), jnp.float32),
            tg,
            tg,
            pltpu.VMEM((2, rows_all, kc), jnp.bfloat16),
            pltpu.VMEM((2, rows_all, kc), jnp.bfloat16),
            pltpu.VMEM((slots, rows_all, CHUNK), jnp.float32),
            pltpu.VMEM((slots, rows_lo, CHUNK), jnp.float32),
            pltpu.VMEM((slots, max(n_hi - 1, 1), rows_d, CHUNK), jnp.float32),
            pltpu.VMEM((slots, rows_d, CHUNK), jnp.float32),
            pltpu.VMEM((late, rows_all // 2, CHUNK), jnp.float32),
            pltpu.VMEM((late, rows_lo // 2, CHUNK), jnp.float32),
            pltpu.VMEM((late, max(n_hi - 1, 1), rows_d // 2, CHUNK), jnp.float32),
            pltpu.VMEM((late, rows_d // 2, CHUNK), jnp.float32),
            dma((2,)),
            dma((2, n_col, ab_rows // CHUNK)),
            dma((n_col, ab_rows // CHUNK)),
            dma((max(n_row - 1, 1),)),
            dma((max(n_row - 1, 1),)),
            dma((slots,)),
            dma((slots,)),
            dma((slots, max(n_hi - 1, 1))),
            dma((slots, max(n_hi - 1, 1))),
            dma((slots, max(n_row - 1, 1))),
            dma((slots, max(n_row - 1, 1))),
            dma((n_depth,)),
            dma((n_depth,)),
            dma((n_depth, max(n_row - 1, 1))),
            dma((n_depth, max(n_row - 1, 1))),
            dma((n_depth, max(n_row - 1, 1))),
            dma((n_depth, max(n_row - 1, 1))),
            dma((late,)),
            dma((late,)),
            dma((late, max(n_hi - 1, 1))),
            dma((late, max(n_hi - 1, 1))),
            dma((late, n_row)),
            dma((late, n_row)),
        ],
        compiler_params=pltpu.CompilerParams(
            collective_id=0, has_side_effects=True, vmem_limit_bytes=60 * 2**20
        ),
        cost_estimate=pl.CostEstimate(
            flops=6 * rows_all * kc * ab_rows * n_col, bytes_accessed=6 * 2**20, transcendentals=0
        ),
    )(integrals, t, order)
    return out.reshape(i_out, j_count // n_row, n_row * n_col * ab_rows)


def solution(mesh):
    sizes = (mesh.shape["row"], mesh.shape["col"], mesh.shape["depth"])
    placed = (P(("row", "col"), "depth"), P("depth", "col", "row"))
    return jax.shard_map(
        functools.partial(shards, sizes),
        mesh=mesh,
        in_specs=placed,
        out_specs=P(("col", "depth"), "row", None),
        check_vma=False,
    )
```

```python
import functools

import jax
import jax.numpy as jnp
import numpy as np
from jax import lax
from jax.experimental import pallas as pl
from jax.experimental.pallas import tpu as pltpu
from jax.sharding import PartitionSpec as P

MESH = pl.DeviceIdType.MESH
CHUNK = 256
LANES = 2


def halves(x):
    hi = x.astype(jnp.bfloat16)
    lo = (x - hi.astype(jnp.float32)).astype(jnp.bfloat16)
    return hi, lo


def kernel(sizes, gathered, w_ref, t_ref, order_ref, out_ref, wg, tg, tg2, th, tl, part, recv1, recv2, fin,
           part_d, recv1_d, recv2_d, fin_d, w_far,
           own_sem, w_send, w_recv, t_send, t_recv, s1_send, s1_recv, s2_send, s2_recv, r_send, r_recv,
           e_send, e_recv, f_send, f_recv, x_send, x_recv, d1_send, d1_recv, d2_send, d2_recv, d_send, d_recv):
    n_row, n_col, n_depth = sizes
    n_lo = LANES
    n_hi = n_depth // n_lo
    ab_rows = w_ref.shape[0]
    n_ch = ab_rows // CHUNK
    assert n_ch == 2 and n_depth == 4 and n_col == 4
    steps = n_col * n_ch
    rows_all = th.shape[1]
    rows_lo = rows_all // n_lo
    rows_d = rows_lo // n_hi
    rows_r = rows_d // n_row
    row, col, depth = lax.axis_index("row"), lax.axis_index("col"), lax.axis_index("depth")
    hi, lo = depth // n_lo, depth % n_lo

    def row_peer(o):
        return (row + o) % n_row

    def hi_peer(o):
        return (hi + o) % n_hi

    mate = hi * n_lo + (1 - lo)
    at_end = (col == 0) | (col == n_col - 1)
    helps = (col == 1) | (col == n_col - 2)
    far = jnp.where(col < n_col // 2, n_col - 1, 0)
    end_col = jnp.where(col < n_col // 2, 0, n_col - 1)
    help_col = jnp.where(col < n_col // 2, 1, n_col - 2)
    normal = jnp.where(at_end, steps - n_ch, steps)

    barrier = pltpu.get_barrier_semaphore()
    for o in range(1, n_row):
        pl.semaphore_signal(barrier, inc=1, device_id={"row": row_peer(o)}, device_id_type=MESH)
    pl.semaphore_signal(barrier, inc=1, device_id={"depth": mate}, device_id_type=MESH)
    for o in range(1, n_hi):
        pl.semaphore_signal(barrier, inc=1, device_id={"depth": hi_peer(o) * n_lo + lo}, device_id_type=MESH)

    @pl.when(col > 0)
    def _():
        pl.semaphore_signal(barrier, inc=1, device_id={"col": col - 1}, device_id_type=MESH)

    @pl.when(col < n_col - 1)
    def _():
        pl.semaphore_signal(barrier, inc=1, device_id={"col": col + 1}, device_id_type=MESH)

    for o in range(1, n_row):

        @pl.when(at_end)
        def _():
            pl.semaphore_signal(
                barrier, inc=1, device_id={"row": row_peer(o), "col": help_col}, device_id_type=MESH
            )

        @pl.when(helps)
        def _():
            pl.semaphore_signal(
                barrier, inc=1, device_id={"row": row_peer(o), "col": end_col}, device_id_type=MESH
            )

    fixed = (n_row - 1) + 1 + (n_hi - 1)
    ends = jnp.where(col > 0, 1, 0) + jnp.where(col < n_col - 1, 1, 0)
    diagonal = jnp.where(at_end | helps, n_row - 1, 0)
    pl.semaphore_wait(barrier, fixed + ends + diagonal)

    def w_copy(src, b, h, side):
        rows = pl.ds(pl.multiple_of(h * CHUNK, CHUNK), CHUNK)
        to = jnp.clip(col + (1 if side else -1), 0, n_col - 1)
        return pltpu.make_async_remote_copy(
            src_ref=w_ref.at[rows] if src is None else wg.at[b, rows],
            dst_ref=wg.at[b, rows],
            send_sem=w_send.at[side, b, h],
            recv_sem=w_recv.at[b, h],
            device_id={"col": to},
            device_id_type=MESH,
        )

    def own_sends(act, h):
        @pl.when(col > 0)
        def _():
            getattr(w_copy(None, col, h, 0), act)()

        @pl.when(col < n_col - 1)
        def _():
            getattr(w_copy(None, col, h, 1), act)()

    def near_sends(act, h):
        @pl.when((col > 0) & goes_right(col - 1))
        def _():
            getattr(w_copy(wg, col - 1, h, 1), act)()

        @pl.when((col < n_col - 1) & goes_left(col + 1))
        def _():
            getattr(w_copy(wg, col + 1, h, 0), act)()

    def near_arrive(h):
        @pl.when(col > 0)
        def _():
            w_copy(wg, col - 1, h, 0).wait_recv()

        @pl.when(col < n_col - 1)
        def _():
            w_copy(wg, col + 1, h, 0).wait_recv()

    def goes_right(b):
        return (col < n_col - 1) & ((b > 0) | (col < n_col - 2))

    def goes_left(b):
        return (col > 0) & ((b < n_col - 1) | (col > 1))

    own_sends("start", 0)

    def t_copy(o):
        return pltpu.make_async_remote_copy(
            src_ref=t_ref,
            dst_ref=tg.at[row],
            send_sem=t_send.at[o - 1],
            recv_sem=t_recv.at[o - 1],
            device_id={"row": row_peer(o)},
            device_id_type=MESH,
        )

    if not gathered:
        for o in range(1, n_row):
            t_copy(o).start()
        t_own = pltpu.make_async_copy(t_ref, tg.at[row], own_sem.at[1])
    else:
        t_own = pltpu.make_async_copy(t_ref, tg, own_sem.at[1])
    t_own.start()
    w_own = pltpu.make_async_copy(w_ref, wg.at[col], own_sem.at[0])
    w_own.start()

    def place(src, q):
        i_out, j_local, kc = t_ref.shape[1:]
        per_r = j_local // n_row
        order = order_ref[...]

        def body(d, c):
            x = src[q, d].reshape(i_out * j_local, kc)
            base = (d % n_lo) * rows_lo + (d // n_lo) * rows_d
            for x_part, into in zip(halves(x), (th, tl)):
                y = jnp.dot(order, x_part, preferred_element_type=jnp.float32).astype(jnp.bfloat16)
                for n in range(n_row * i_out):
                    at = base + n * (per_r * n_row) + q * per_r
                    into[0, pl.ds(pl.multiple_of(at, per_r), per_r), :] = y[n * per_r : (n + 1) * per_r]
            return c

        lax.fori_loop(0, n_depth, body, 0)

    def place_piece(q, p):
        i_out, j_local, kc = t_ref.shape[1:]
        per_r = j_local // n_row
        x = tg2[q, :, p].reshape(n_depth * j_local, kc)
        for x_part, into in zip(halves(x), (th, tl)):
            y = jnp.dot(order_ref[...], x_part, preferred_element_type=jnp.float32).astype(jnp.bfloat16)
            for n in range(n_row * n_depth):
                r, d = n // n_depth, n % n_depth
                base = p * rows_all + (d % n_lo) * rows_lo + (d // n_lo) * rows_d + r * rows_r
                at = base // n_depth + q * per_r
                into[1, pl.ds(pl.multiple_of(at, per_r), per_r), :] = y[n * per_r : (n + 1) * per_r]

    def plain_groups():
        for d in range(n_depth):
            base = (d % n_lo) * rows_lo + (d // n_lo) * rows_d
            x = tg2[pl.ds(base, rows_d), :].reshape(n_row, 2, rows_r // 2, -1)
            for g in range(2):
                at = pl.ds((g * rows_all + base) // 2, rows_d // 2)
                th[1, at, :], tl[1, at, :] = halves(x[:, g].reshape(rows_d // 2, -1))

    def plain():
        def body(m, c):
            at = pl.ds(pl.multiple_of(m * 64, 64), 64)
            th[0, at, :], tl[0, at, :] = halves(tg[at, :])
            return c

        lax.fori_loop(0, rows_all // 64, body, 0)

    piece = rows_all // n_depth
    n_swap = n_depth // 2
    n_g = 2 if gathered else n_depth

    def e_copy(p):
        rows = pl.ds(p * piece, piece)
        return pltpu.make_async_remote_copy(
            src_ref=t_ref.at[rows] if gathered else t_ref.at[:, p],
            dst_ref=tg2.at[rows] if gathered else tg2.at[row, :, p],
            send_sem=e_send.at[p],
            recv_sem=e_recv.at[p],
            device_id={"col": help_col},
            device_id_type=MESH,
        )

    def x_copy(p, o):
        return pltpu.make_async_remote_copy(
            src_ref=tg2.at[row, :, p],
            dst_ref=tg2.at[row, :, p],
            send_sem=x_send.at[p, o - 1],
            recv_sem=x_recv.at[p, o - 1],
            device_id={"row": row_peer(o)},
            device_id_type=MESH,
        )

    def f_copy(p, o):
        q = (row + n_row - o) % n_row
        return pltpu.make_async_remote_copy(
            src_ref=tg.at[q, :, p],
            dst_ref=tg2.at[q, :, p],
            send_sem=f_send.at[p, o - 1],
            recv_sem=f_recv.at[p, o - 1],
            device_id={"col": help_col},
            device_id_type=MESH,
        )

    def take(p):
        e_copy(p).wait_recv()
        if not gathered and p < n_swap:
            for o in range(1, n_row):
                x_copy(p, o).start()

    def place_own(p):
        if not gathered:
            place_piece(row, p)

    def place_peers(p):
        if not gathered:
            for o in range(1, n_row):
                (x_copy if p < n_swap else f_copy)(p, o).wait_recv()
                place_piece((row + n_row - o) % n_row, p)

    t_own.wait()
    if not gathered:
        place(tg, row)
    else:
        plain()

    own_sends("wait_send", 0)
    own_sends("start", 1)
    near_arrive(0)
    own_sends("wait_send", 1)
    near_sends("start", 0)

    @pl.when(at_end)
    def _():
        e_copy(0).start()
        e_copy(1).start()

    near_arrive(1)
    if not gathered:
        for o in range(1, n_row):
            t_copy(o).wait_recv()
            place(tg, (row + n_row - o) % n_row)
    w_own.wait()

    near = jnp.minimum(col, n_col - 1 - col)

    def block_at(k):
        p, h = k // n_ch, k % n_ch
        both = p <= 2 * near
        s = jnp.where(both, (p + 1) // 2, p - near)
        left = jnp.where(both, p % 2 == 1, col > near)
        b = jnp.where(p == 0, col, jnp.where(left, col - s, col + s))
        return b, h, s

    def s1_copy(k):
        return pltpu.make_async_remote_copy(
            src_ref=part.at[k, pl.ds(pl.multiple_of((1 - lo) * rows_lo, rows_lo), rows_lo)],
            dst_ref=recv1.at[k],
            send_sem=s1_send.at[k],
            recv_sem=s1_recv.at[k],
            device_id={"depth": mate},
            device_id_type=MESH,
        )

    def s2_copy(k, o):
        return pltpu.make_async_remote_copy(
            src_ref=part.at[k, pl.ds(pl.multiple_of(lo * rows_lo + hi_peer(o) * rows_d, rows_d), rows_d)],
            dst_ref=recv2.at[k, o - 1],
            send_sem=s2_send.at[k, o - 1],
            recv_sem=s2_recv.at[k, o - 1],
            device_id={"depth": hi_peer(o) * n_lo + lo},
            device_id_type=MESH,
        )

    def out_cols(b, h):
        return pl.ds(pl.multiple_of((row * n_col + b) * ab_rows + h * CHUNK, CHUNK), CHUNK)

    def r_copy(k, o):
        return pltpu.make_async_remote_copy(
            src_ref=fin.at[k, pl.ds(pl.multiple_of(row_peer(o) * rows_r, rows_r), rows_r)],
            dst_ref=out_ref.at[:, out_cols(*block_at(k)[:2])],
            send_sem=r_send.at[k, o - 1],
            recv_sem=r_recv.at[k, o - 1],
            device_id={"row": row_peer(o)},
            device_id_type=MESH,
        )

    def d1_copy(n):
        return pltpu.make_async_remote_copy(
            src_ref=part_d.at[n, pl.ds(pl.multiple_of((1 - lo) * (rows_lo // n_g), rows_lo // n_g), rows_lo // n_g)],
            dst_ref=recv1_d.at[n],
            send_sem=d1_send.at[n],
            recv_sem=d1_recv.at[n],
            device_id={"depth": mate},
            device_id_type=MESH,
        )

    def d2_copy(n, o):
        start = lo * (rows_lo // n_g) + hi_peer(o) * (rows_d // n_g)
        return pltpu.make_async_remote_copy(
            src_ref=part_d.at[n, pl.ds(pl.multiple_of(start, rows_d // n_g), rows_d // n_g)],
            dst_ref=recv2_d.at[n, o - 1],
            send_sem=d2_send.at[n, o - 1],
            recv_sem=d2_recv.at[n, o - 1],
            device_id={"depth": hi_peer(o) * n_lo + lo},
            device_id_type=MESH,
        )

    def d_copy(n, o):
        g, h = n // n_ch, n % n_ch
        half = rows_r // n_g
        return pltpu.make_async_remote_copy(
            src_ref=fin_d.at[n, pl.ds(pl.multiple_of(row_peer(o) * half, half), half)],
            dst_ref=out_ref.at[pl.ds(g * half, half), out_cols(far, h)],
            send_sem=d_send.at[n, o],
            recv_sem=d_recv.at[n, o],
            device_id={"row": row_peer(o), "col": end_col},
            device_id_type=MESH,
        )

    def multiply(w_halves, which, first, tile):
        wh, wl = w_halves
        w3 = jnp.concatenate([wh, wh, wl], axis=0)
        for start in first:
            at = pl.ds(start, tile)
            a = th[which, at, :]
            a3 = jnp.concatenate([a, tl[which, at, :], a], axis=1)
            yield start, jnp.dot(a3, w3, preferred_element_type=jnp.float32)

    def d_multiply(n):
        rows = rows_all // n_g
        h = n % n_ch
        for _, y in multiply((w_far[h, 0], w_far[h, 1]), 1, (n // n_ch * rows,), rows):
            part_d[n] = y
        d1_copy(n).start()

    def d_pair(n):
        d1_copy(n).wait_recv()
        at = pl.ds(pl.multiple_of(lo * (rows_lo // n_g), rows_lo // n_g), rows_lo // n_g)
        part_d[n, at, :] = part_d[n, at, :] + recv1_d[n]
        for o in range(1, n_hi):
            d2_copy(n, o).start()

    def d_finish(n):
        start = lo * (rows_lo // n_g) + hi * (rows_d // n_g)
        total = part_d[n, pl.ds(pl.multiple_of(start, rows_d // n_g), rows_d // n_g), :]
        for o in range(1, n_hi):
            d2_copy(n, o).wait_recv()
            total = total + recv2_d[n, o - 1]
        fin_d[n] = total
        for o in range(n_row):
            d_copy(n, o).start()

    def pair(j):
        s1_copy(j).wait_recv()
        at = pl.ds(pl.multiple_of(lo * rows_lo, rows_lo), rows_lo)
        part[j, at, :] = part[j, at, :] + recv1[j]
        for o in range(1, n_hi):
            s2_copy(j, o).start()

    def finish(j):
        total = part[j, pl.ds(pl.multiple_of(lo * rows_lo + hi * rows_d, rows_d), rows_d), :]
        for o in range(1, n_hi):
            s2_copy(j, o).wait_recv()
            total = total + recv2[j, o - 1]
        fin[j] = total
        for o in range(1, n_row):
            r_copy(j, o).start()
        mine = fin[j, pl.ds(pl.multiple_of(row * rows_r, rows_r), rows_r), :]
        out_ref[:, out_cols(*block_at(j)[:2])] = mine

    def step(k, c):
        @pl.when(helps & (k == 1))
        def _():
            take(0)

        @pl.when(helps & (k == 3))
        def _():
            take(1)

        @pl.when(helps & (k == steps - 1))
        def _():
            place_own(0)
            place_own(1)
            place_peers(0)

        @pl.when(k == 3)
        def _():
            near_sends("wait_send", 0)
            near_sends("start", 1)

        for p in range(n_swap, n_depth):

            @pl.when(at_end & (k == 2 * (p - n_swap)))
            def _():
                e_copy(p - n_swap).wait_send()
                e_copy(p).start()
                if not gathered:
                    for o in range(1, n_row):
                        f_copy(p, o).start()

        b, h, s = block_at(k)

        @pl.when(s >= 2)
        def _():
            w_copy(wg, b, h, 0).wait_recv()

        w_halves = halves(wg[b, pl.ds(pl.multiple_of(h * CHUNK, CHUNK), CHUNK), :].T)

        @pl.when(helps & (k >= steps - n_ch))
        def _():
            w_far[h, 0], w_far[h, 1] = w_halves

        for start, y in multiply(w_halves, 0, (0, rows_all // 2), rows_all // 2):
            part[k, pl.ds(start, rows_all // 2), :] = y
        s1_copy(k).start()

        @pl.when(k >= 1)
        def _():
            pair(k - 1)

        @pl.when(k >= 2)
        def _():
            finish(k - 2)

        return c

    lax.fori_loop(0, normal, step, 0)

    def group(act, g):
        for h in range(n_ch):
            act(g * n_ch + h)

    @pl.when(helps)
    def _():
        place_peers(1)
        if gathered:
            for p in range(n_swap, n_depth):
                take(p)
            plain_groups()
        group(d_multiply, 0)

    pair(normal - 1)
    finish(normal - 2)

    @pl.when(helps)
    def _():
        group(d_multiply, 1)
        group(d_pair, 0)

    finish(normal - 1)

    @pl.when(helps)
    def _():
        group(d_pair, 1)
        group(d_finish, 0)
        group(d_finish, 1)
        for g in range(2, n_g):
            take(g)
            place_own(g)
            place_peers(g)
            group(d_multiply, g)
            if g > 2:
                group(d_finish, g - 1)
            group(d_pair, g)
        if n_g > 2:
            group(d_finish, n_g - 1)

    def drain(k, c):
        s1_copy(k).wait_send()
        for o in range(1, n_hi):
            s2_copy(k, o).wait_send()
        for o in range(1, n_row):
            r_copy(k, o).wait_send()
            r_copy(k, o).wait_recv()
        return c

    lax.fori_loop(0, normal, drain, 0)

    @pl.when(helps)
    def _():
        for n in range(n_g * n_ch):
            d1_copy(n).wait_send()
            for o in range(1, n_hi):
                d2_copy(n, o).wait_send()
            for o in range(n_row):
                d_copy(n, o).wait_send()

    near_sends("wait_send", 1)

    @pl.when(at_end)
    def _():
        for p in range(n_swap, n_depth):
            e_copy(p).wait_send()
            if not gathered:
                for o in range(1, n_row):
                    f_copy(p, o).wait_send()
        for n in range(n_g * n_ch):
            for o in range(n_row):
                d_copy(n, o).wait_recv()

    if not gathered:

        @pl.when(helps)
        def _():
            for p in range(n_swap):
                for o in range(1, n_row):
                    x_copy(p, o).wait_send()

    if not gathered:
        for o in range(1, n_row):
            t_copy(o).wait_send()


def shards(sizes, integrals, amplitudes):
    n_row, n_col, n_depth = sizes
    n_lo = LANES
    n_hi = n_depth // n_lo
    kc, i_count, j_local = amplitudes.shape
    j_count = j_local * n_row
    ab_rows = integrals.shape[0]
    n_ch = ab_rows // CHUNK
    slots = n_col * n_ch
    n_g = 2 if j_local % (16 * n_row) != 0 else n_depth
    late = n_g * n_ch
    rows_all = i_count * j_count
    rows_lo = rows_all // n_lo
    rows_d = rows_lo // n_hi
    rows_r = rows_d // n_row
    i_out = i_count // n_depth
    gathered = j_local % (16 * n_row) != 0
    side = i_out * j_local
    tiny = j_local if gathered else n_row
    source = np.arange(side).reshape(i_out, j_local // tiny, tiny).transpose(2, 0, 1).reshape(-1)
    order = jnp.asarray(np.eye(side)[source], jnp.bfloat16)
    assert i_out == n_depth
    t = jnp.transpose(amplitudes, (1, 2, 0))
    if gathered:
        t = lax.all_gather(t, "row", axis=1, tiled=True)
        t = t.reshape(n_hi, n_lo, i_out, j_count // n_row, n_row, kc)
        t = jnp.transpose(t, (1, 0, 4, 2, 3, 5)).reshape(rows_all, kc)
        tg = pltpu.VMEM(t.shape, jnp.float32)
    else:
        t = t.reshape(n_depth, i_out, j_local, kc)
        tg = pltpu.VMEM((n_row,) + t.shape, jnp.float32)
    dma = pltpu.SemaphoreType.DMA
    out = pl.pallas_call(
        functools.partial(kernel, sizes, gathered),
        out_shape=jax.ShapeDtypeStruct((rows_r, n_row * n_col * ab_rows), jnp.float32),
        in_specs=[pl.BlockSpec(memory_space=pl.ANY)] * 2 + [pl.BlockSpec(memory_space=pltpu.VMEM)],
        out_specs=pl.BlockSpec(memory_space=pltpu.VMEM),
        scratch_shapes=[
            pltpu.VMEM((n_col, ab_rows, kc), jnp.float32),
            tg,
            tg,
            pltpu.VMEM((2, rows_all, kc), jnp.bfloat16),
            pltpu.VMEM((2, rows_all, kc), jnp.bfloat16),
            pltpu.VMEM((slots, rows_all, CHUNK), jnp.float32),
            pltpu.VMEM((slots, rows_lo, CHUNK), jnp.float32),
            pltpu.VMEM((slots, max(n_hi - 1, 1), rows_d, CHUNK), jnp.float32),
            pltpu.VMEM((slots, rows_d, CHUNK), jnp.float32),
            pltpu.VMEM((late, rows_all // n_g, CHUNK), jnp.float32),
            pltpu.VMEM((late, rows_lo // n_g, CHUNK), jnp.float32),
            pltpu.VMEM((late, max(n_hi - 1, 1), rows_d // n_g, CHUNK), jnp.float32),
            pltpu.VMEM((late, rows_d // n_g, CHUNK), jnp.float32),
            pltpu.VMEM((n_ch, 2, kc, CHUNK), jnp.bfloat16),
            dma((2,)),
            dma((2, n_col, ab_rows // CHUNK)),
            dma((n_col, ab_rows // CHUNK)),
            dma((max(n_row - 1, 1),)),
            dma((max(n_row - 1, 1),)),
            dma((slots,)),
            dma((slots,)),
            dma((slots, max(n_hi - 1, 1))),
            dma((slots, max(n_hi - 1, 1))),
            dma((slots, max(n_row - 1, 1))),
            dma((slots, max(n_row - 1, 1))),
            dma((n_depth,)),
            dma((n_depth,)),
            dma((n_depth, max(n_row - 1, 1))),
            dma((n_depth, max(n_row - 1, 1))),
            dma((n_depth, max(n_row - 1, 1))),
            dma((n_depth, max(n_row - 1, 1))),
            dma((late,)),
            dma((late,)),
            dma((late, max(n_hi - 1, 1))),
            dma((late, max(n_hi - 1, 1))),
            dma((late, n_row)),
            dma((late, n_row)),
        ],
        compiler_params=pltpu.CompilerParams(
            collective_id=0, has_side_effects=True, vmem_limit_bytes=60 * 2**20
        ),
        cost_estimate=pl.CostEstimate(
            flops=6 * rows_all * kc * ab_rows * n_col, bytes_accessed=6 * 2**20, transcendentals=0
        ),
    )(integrals, t, order)
    return out.reshape(i_out, j_count // n_row, n_row * n_col * ab_rows)


def solution(mesh):
    sizes = (mesh.shape["row"], mesh.shape["col"], mesh.shape["depth"])
    placed = (P(("row", "col"), "depth"), P("depth", "col", "row"))
    return jax.shard_map(
        functools.partial(shards, sizes),
        mesh=mesh,
        in_specs=placed,
        out_specs=P(("col", "depth"), "row", None),
        check_vma=False,
    )
```

```python
import functools

import jax
import jax.numpy as jnp
import numpy as np
from jax import lax
from jax.experimental import pallas as pl
from jax.experimental.pallas import tpu as pltpu
from jax.sharding import PartitionSpec as P

MESH = pl.DeviceIdType.MESH
CHUNK = 256
LANES = 2


def halves(x):
    hi = x.astype(jnp.bfloat16)
    lo = (x - hi.astype(jnp.float32)).astype(jnp.bfloat16)
    return hi, lo


def kernel(sizes, gathered, w_ref, t_ref, order_ref, out_ref, wg, tg, tg2, th, tl, part, recv1, recv2, fin,
           part_d, recv1_d, recv2_d, fin_d, w_far,
           own_sem, w_send, w_recv, t_send, t_recv, s1_send, s1_recv, s2_send, s2_recv, r_send, r_recv,
           e_send, e_recv, f_send, f_recv, x_send, x_recv, d1_send, d1_recv, d2_send, d2_recv, d_send, d_recv):
    n_row, n_col, n_depth = sizes
    n_lo = LANES
    n_hi = n_depth // n_lo
    ab_rows = w_ref.shape[0]
    n_ch = ab_rows // CHUNK
    assert n_ch == 2 and n_depth == 4 and n_col == 4
    steps = n_col * n_ch
    rows_all = th.shape[1]
    rows_lo = rows_all // n_lo
    rows_d = rows_lo // n_hi
    rows_r = rows_d // n_row
    row, col, depth = lax.axis_index("row"), lax.axis_index("col"), lax.axis_index("depth")
    hi, lo = depth // n_lo, depth % n_lo

    def row_peer(o):
        return (row + o) % n_row

    def hi_peer(o):
        return (hi + o) % n_hi

    mate = hi * n_lo + (1 - lo)
    at_end = (col == 0) | (col == n_col - 1)
    helps = (col == 1) | (col == n_col - 2)
    far = jnp.where(col < n_col // 2, n_col - 1, 0)
    end_col = jnp.where(col < n_col // 2, 0, n_col - 1)
    help_col = jnp.where(col < n_col // 2, 1, n_col - 2)
    normal = jnp.where(at_end, steps - n_ch, steps)

    barrier = pltpu.get_barrier_semaphore()
    for o in range(1, n_row):
        pl.semaphore_signal(barrier, inc=1, device_id={"row": row_peer(o)}, device_id_type=MESH)
    pl.semaphore_signal(barrier, inc=1, device_id={"depth": mate}, device_id_type=MESH)
    for o in range(1, n_hi):
        pl.semaphore_signal(barrier, inc=1, device_id={"depth": hi_peer(o) * n_lo + lo}, device_id_type=MESH)

    @pl.when(col > 0)
    def _():
        pl.semaphore_signal(barrier, inc=1, device_id={"col": col - 1}, device_id_type=MESH)

    @pl.when(col < n_col - 1)
    def _():
        pl.semaphore_signal(barrier, inc=1, device_id={"col": col + 1}, device_id_type=MESH)

    for o in range(1, n_row):

        @pl.when(at_end)
        def _():
            pl.semaphore_signal(
                barrier, inc=1, device_id={"row": row_peer(o), "col": help_col}, device_id_type=MESH
            )

        @pl.when(helps)
        def _():
            pl.semaphore_signal(
                barrier, inc=1, device_id={"row": row_peer(o), "col": end_col}, device_id_type=MESH
            )

    fixed = (n_row - 1) + 1 + (n_hi - 1)
    ends = jnp.where(col > 0, 1, 0) + jnp.where(col < n_col - 1, 1, 0)
    diagonal = jnp.where(at_end | helps, n_row - 1, 0)
    pl.semaphore_wait(barrier, fixed + ends + diagonal)

    def w_copy(src, b, h, side):
        rows = pl.ds(pl.multiple_of(h * CHUNK, CHUNK), CHUNK)
        to = jnp.clip(col + (1 if side else -1), 0, n_col - 1)
        return pltpu.make_async_remote_copy(
            src_ref=w_ref.at[rows] if src is None else wg.at[b, rows],
            dst_ref=wg.at[b, rows],
            send_sem=w_send.at[side, b, h],
            recv_sem=w_recv.at[b, h],
            device_id={"col": to},
            device_id_type=MESH,
        )

    def own_sends(act, h):
        @pl.when(col > 0)
        def _():
            getattr(w_copy(None, col, h, 0), act)()

        @pl.when(col < n_col - 1)
        def _():
            getattr(w_copy(None, col, h, 1), act)()

    def near_sends(act, h):
        @pl.when((col > 0) & goes_right(col - 1))
        def _():
            getattr(w_copy(wg, col - 1, h, 1), act)()

        @pl.when((col < n_col - 1) & goes_left(col + 1))
        def _():
            getattr(w_copy(wg, col + 1, h, 0), act)()

    def near_arrive(h):
        @pl.when(col > 0)
        def _():
            w_copy(wg, col - 1, h, 0).wait_recv()

        @pl.when(col < n_col - 1)
        def _():
            w_copy(wg, col + 1, h, 0).wait_recv()

    def goes_right(b):
        return (col < n_col - 1) & ((b > 0) | (col < n_col - 2))

    def goes_left(b):
        return (col > 0) & ((b < n_col - 1) | (col > 1))

    own_sends("start", 0)

    def t_copy(o, d):
        return pltpu.make_async_remote_copy(
            src_ref=t_ref.at[d],
            dst_ref=tg.at[row, d],
            send_sem=t_send.at[o - 1, d],
            recv_sem=t_recv.at[o - 1, d],
            device_id={"row": row_peer(o)},
            device_id_type=MESH,
        )

    if not gathered:
        for d in range(n_depth):
            for o in range(1, n_row):
                t_copy(o, d).start()
        t_own = pltpu.make_async_copy(t_ref, tg.at[row], own_sem.at[1])
    else:
        t_own = pltpu.make_async_copy(t_ref, tg, own_sem.at[1])
    t_own.start()
    w_own = pltpu.make_async_copy(w_ref, wg.at[col], own_sem.at[0])
    w_own.start()

    def place(src, q, first, last):
        i_out, j_local, kc = t_ref.shape[1:]
        per_r = j_local // n_row
        order = order_ref[...]

        def body(d, c):
            x = src[q, d].reshape(i_out * j_local, kc)
            base = (d % n_lo) * rows_lo + (d // n_lo) * rows_d
            for x_part, into in zip(halves(x), (th, tl)):
                y = jnp.dot(order, x_part, preferred_element_type=jnp.float32).astype(jnp.bfloat16)
                for n in range(n_row * i_out):
                    at = base + n * (per_r * n_row) + q * per_r
                    into[0, pl.ds(pl.multiple_of(at, per_r), per_r), :] = y[n * per_r : (n + 1) * per_r]
            return c

        lax.fori_loop(first, last, body, 0)

    def place_piece(q, p):
        i_out, j_local, kc = t_ref.shape[1:]
        per_r = j_local // n_row
        x = tg2[q, :, p].reshape(n_depth * j_local, kc)
        for x_part, into in zip(halves(x), (th, tl)):
            y = jnp.dot(order_ref[...], x_part, preferred_element_type=jnp.float32).astype(jnp.bfloat16)
            for n in range(n_row * n_depth):
                r, d = n // n_depth, n % n_depth
                base = p * rows_all + (d % n_lo) * rows_lo + (d // n_lo) * rows_d + r * rows_r
                at = base // n_depth + q * per_r
                into[1, pl.ds(pl.multiple_of(at, per_r), per_r), :] = y[n * per_r : (n + 1) * per_r]

    def plain_groups():
        for d in range(n_depth):
            base = (d % n_lo) * rows_lo + (d // n_lo) * rows_d
            x = tg2[pl.ds(base, rows_d), :].reshape(n_row, 2, rows_r // 2, -1)
            for g in range(2):
                at = pl.ds((g * rows_all + base) // 2, rows_d // 2)
                th[1, at, :], tl[1, at, :] = halves(x[:, g].reshape(rows_d // 2, -1))

    def plain():
        def body(m, c):
            at = pl.ds(pl.multiple_of(m * 64, 64), 64)
            th[0, at, :], tl[0, at, :] = halves(tg[at, :])
            return c

        lax.fori_loop(0, rows_all // 64, body, 0)

    piece = rows_all // n_depth
    n_swap = n_depth // 2
    n_g = 2 if gathered else n_depth

    def e_copy(p):
        rows = pl.ds(p * piece, piece)
        return pltpu.make_async_remote_copy(
            src_ref=t_ref.at[rows] if gathered else t_ref.at[:, p],
            dst_ref=tg2.at[rows] if gathered else tg2.at[row, :, p],
            send_sem=e_send.at[p],
            recv_sem=e_recv.at[p],
            device_id={"col": help_col},
            device_id_type=MESH,
        )

    def x_copy(p, o):
        return pltpu.make_async_remote_copy(
            src_ref=tg2.at[row, :, p],
            dst_ref=tg2.at[row, :, p],
            send_sem=x_send.at[p, o - 1],
            recv_sem=x_recv.at[p, o - 1],
            device_id={"row": row_peer(o)},
            device_id_type=MESH,
        )

    def f_copy(p, o):
        q = (row + n_row - o) % n_row
        return pltpu.make_async_remote_copy(
            src_ref=tg.at[q, :, p],
            dst_ref=tg2.at[q, :, p],
            send_sem=f_send.at[p, o - 1],
            recv_sem=f_recv.at[p, o - 1],
            device_id={"col": help_col},
            device_id_type=MESH,
        )

    def take(p):
        e_copy(p).wait_recv()
        if not gathered and p < n_swap:
            for o in range(1, n_row):
                x_copy(p, o).start()

    def place_own(p):
        if not gathered:
            place_piece(row, p)

    def place_peers(p):
        if not gathered:
            for o in range(1, n_row):
                (x_copy if p < n_swap else f_copy)(p, o).wait_recv()
                place_piece((row + n_row - o) % n_row, p)

    t_own.wait()
    if not gathered:
        place(tg, row, 0, n_depth)
    else:
        plain()

    own_sends("wait_send", 0)
    own_sends("start", 1)
    near_arrive(0)
    own_sends("wait_send", 1)
    near_sends("start", 0)

    @pl.when(at_end)
    def _():
        e_copy(0).start()
        e_copy(1).start()

    near_arrive(1)
    if not gathered:
        for d in range(n_depth):
            for o in range(1, n_row):
                t_copy(o, d).wait_recv()
                place(tg, (row + n_row - o) % n_row, d, d + 1)
    w_own.wait()

    near = jnp.minimum(col, n_col - 1 - col)

    def block_at(k):
        p, h = k // n_ch, k % n_ch
        both = p <= 2 * near
        s = jnp.where(both, (p + 1) // 2, p - near)
        left = jnp.where(both, p % 2 == 1, col > near)
        b = jnp.where(p == 0, col, jnp.where(left, col - s, col + s))
        return b, h, s

    def s1_copy(k):
        return pltpu.make_async_remote_copy(
            src_ref=part.at[k, pl.ds(pl.multiple_of((1 - lo) * rows_lo, rows_lo), rows_lo)],
            dst_ref=recv1.at[k],
            send_sem=s1_send.at[k],
            recv_sem=s1_recv.at[k],
            device_id={"depth": mate},
            device_id_type=MESH,
        )

    def s2_copy(k, o):
        return pltpu.make_async_remote_copy(
            src_ref=part.at[k, pl.ds(pl.multiple_of(lo * rows_lo + hi_peer(o) * rows_d, rows_d), rows_d)],
            dst_ref=recv2.at[k, o - 1],
            send_sem=s2_send.at[k, o - 1],
            recv_sem=s2_recv.at[k, o - 1],
            device_id={"depth": hi_peer(o) * n_lo + lo},
            device_id_type=MESH,
        )

    def out_cols(b, h):
        return pl.ds(pl.multiple_of((row * n_col + b) * ab_rows + h * CHUNK, CHUNK), CHUNK)

    def r_copy(k, o):
        return pltpu.make_async_remote_copy(
            src_ref=fin.at[k, pl.ds(pl.multiple_of(row_peer(o) * rows_r, rows_r), rows_r)],
            dst_ref=out_ref.at[:, out_cols(*block_at(k)[:2])],
            send_sem=r_send.at[k, o - 1],
            recv_sem=r_recv.at[k, o - 1],
            device_id={"row": row_peer(o)},
            device_id_type=MESH,
        )

    def d1_copy(n):
        return pltpu.make_async_remote_copy(
            src_ref=part_d.at[n, pl.ds(pl.multiple_of((1 - lo) * (rows_lo // n_g), rows_lo // n_g), rows_lo // n_g)],
            dst_ref=recv1_d.at[n],
            send_sem=d1_send.at[n],
            recv_sem=d1_recv.at[n],
            device_id={"depth": mate},
            device_id_type=MESH,
        )

    def d2_copy(n, o):
        start = lo * (rows_lo // n_g) + hi_peer(o) * (rows_d // n_g)
        return pltpu.make_async_remote_copy(
            src_ref=part_d.at[n, pl.ds(pl.multiple_of(start, rows_d // n_g), rows_d // n_g)],
            dst_ref=recv2_d.at[n, o - 1],
            send_sem=d2_send.at[n, o - 1],
            recv_sem=d2_recv.at[n, o - 1],
            device_id={"depth": hi_peer(o) * n_lo + lo},
            device_id_type=MESH,
        )

    def d_copy(n, o):
        g, h = n // n_ch, n % n_ch
        half = rows_r // n_g
        return pltpu.make_async_remote_copy(
            src_ref=fin_d.at[n, pl.ds(pl.multiple_of(row_peer(o) * half, half), half)],
            dst_ref=out_ref.at[pl.ds(g * half, half), out_cols(far, h)],
            send_sem=d_send.at[n, o],
            recv_sem=d_recv.at[n, o],
            device_id={"row": row_peer(o), "col": end_col},
            device_id_type=MESH,
        )

    def multiply(w_halves, which, first, tile):
        wh, wl = w_halves
        w3 = jnp.concatenate([wh, wh, wl], axis=0)
        for start in first:
            at = pl.ds(start, tile)
            a = th[which, at, :]
            a3 = jnp.concatenate([a, tl[which, at, :], a], axis=1)
            yield start, jnp.dot(a3, w3, preferred_element_type=jnp.float32)

    def d_multiply(n):
        rows = rows_all // n_g
        h = n % n_ch
        for _, y in multiply((w_far[h, 0], w_far[h, 1]), 1, (n // n_ch * rows,), rows):
            part_d[n] = y
        d1_copy(n).start()

    def d_pair(n):
        d1_copy(n).wait_recv()
        at = pl.ds(pl.multiple_of(lo * (rows_lo // n_g), rows_lo // n_g), rows_lo // n_g)
        part_d[n, at, :] = part_d[n, at, :] + recv1_d[n]
        for o in range(1, n_hi):
            d2_copy(n, o).start()

    def d_finish(n):
        start = lo * (rows_lo // n_g) + hi * (rows_d // n_g)
        total = part_d[n, pl.ds(pl.multiple_of(start, rows_d // n_g), rows_d // n_g), :]
        for o in range(1, n_hi):
            d2_copy(n, o).wait_recv()
            total = total + recv2_d[n, o - 1]
        fin_d[n] = total
        for o in range(n_row):
            d_copy(n, o).start()

    def pair(j):
        s1_copy(j).wait_recv()
        at = pl.ds(pl.multiple_of(lo * rows_lo, rows_lo), rows_lo)
        part[j, at, :] = part[j, at, :] + recv1[j]
        for o in range(1, n_hi):
            s2_copy(j, o).start()

    def finish(j):
        total = part[j, pl.ds(pl.multiple_of(lo * rows_lo + hi * rows_d, rows_d), rows_d), :]
        for o in range(1, n_hi):
            s2_copy(j, o).wait_recv()
            total = total + recv2[j, o - 1]
        fin[j] = total
        for o in range(1, n_row):
            r_copy(j, o).start()
        mine = fin[j, pl.ds(pl.multiple_of(row * rows_r, rows_r), rows_r), :]
        out_ref[:, out_cols(*block_at(j)[:2])] = mine

    def step(k, c):
        @pl.when(helps & (k == 1))
        def _():
            take(0)

        @pl.when(helps & (k == 3))
        def _():
            take(1)

        @pl.when(helps & (k == steps - 1))
        def _():
            place_own(0)
            place_own(1)
            place_peers(0)

        @pl.when(k == 3)
        def _():
            near_sends("wait_send", 0)
            near_sends("start", 1)

        for p in range(n_swap, n_depth):

            @pl.when(at_end & (k == 2 * (p - n_swap)))
            def _():
                e_copy(p - n_swap).wait_send()
                e_copy(p).start()
                if not gathered:
                    for o in range(1, n_row):
                        f_copy(p, o).start()

        b, h, s = block_at(k)

        @pl.when(s >= 2)
        def _():
            w_copy(wg, b, h, 0).wait_recv()

        w_halves = halves(wg[b, pl.ds(pl.multiple_of(h * CHUNK, CHUNK), CHUNK), :].T)

        @pl.when(helps & (k >= steps - n_ch))
        def _():
            w_far[h, 0], w_far[h, 1] = w_halves

        for start, y in multiply(w_halves, 0, (0, rows_all // 2), rows_all // 2):
            part[k, pl.ds(start, rows_all // 2), :] = y
        s1_copy(k).start()

        @pl.when(k >= 1)
        def _():
            pair(k - 1)

        @pl.when(k >= 2)
        def _():
            finish(k - 2)

        return c

    lax.fori_loop(0, normal, step, 0)

    def group(act, g):
        for h in range(n_ch):
            act(g * n_ch + h)

    @pl.when(helps)
    def _():
        place_peers(1)
        if gathered:
            for p in range(n_swap, n_depth):
                take(p)
            plain_groups()
        group(d_multiply, 0)

    pair(normal - 1)
    finish(normal - 2)

    @pl.when(helps)
    def _():
        group(d_multiply, 1)
        group(d_pair, 0)

    finish(normal - 1)

    @pl.when(helps)
    def _():
        group(d_pair, 1)
        group(d_finish, 0)
        group(d_finish, 1)
        for g in range(2, n_g):
            take(g)
            place_own(g)
            place_peers(g)
            group(d_multiply, g)
            if g > 2:
                group(d_finish, g - 1)
            group(d_pair, g)
        if n_g > 2:
            group(d_finish, n_g - 1)

    def drain(k, c):
        s1_copy(k).wait_send()
        for o in range(1, n_hi):
            s2_copy(k, o).wait_send()
        for o in range(1, n_row):
            r_copy(k, o).wait_send()
            r_copy(k, o).wait_recv()
        return c

    lax.fori_loop(0, normal, drain, 0)

    @pl.when(helps)
    def _():
        for n in range(n_g * n_ch):
            d1_copy(n).wait_send()
            for o in range(1, n_hi):
                d2_copy(n, o).wait_send()
            for o in range(n_row):
                d_copy(n, o).wait_send()

    near_sends("wait_send", 1)

    @pl.when(at_end)
    def _():
        for p in range(n_swap, n_depth):
            e_copy(p).wait_send()
            if not gathered:
                for o in range(1, n_row):
                    f_copy(p, o).wait_send()
        for n in range(n_g * n_ch):
            for o in range(n_row):
                d_copy(n, o).wait_recv()

    if not gathered:

        @pl.when(helps)
        def _():
            for p in range(n_swap):
                for o in range(1, n_row):
                    x_copy(p, o).wait_send()

    if not gathered:
        for d in range(n_depth):
            for o in range(1, n_row):
                t_copy(o, d).wait_send()


def shards(sizes, integrals, amplitudes):
    n_row, n_col, n_depth = sizes
    n_lo = LANES
    n_hi = n_depth // n_lo
    kc, i_count, j_local = amplitudes.shape
    j_count = j_local * n_row
    ab_rows = integrals.shape[0]
    n_ch = ab_rows // CHUNK
    slots = n_col * n_ch
    n_g = 2 if j_local % (16 * n_row) != 0 else n_depth
    late = n_g * n_ch
    rows_all = i_count * j_count
    rows_lo = rows_all // n_lo
    rows_d = rows_lo // n_hi
    rows_r = rows_d // n_row
    i_out = i_count // n_depth
    gathered = j_local % (16 * n_row) != 0
    side = i_out * j_local
    tiny = j_local if gathered else n_row
    source = np.arange(side).reshape(i_out, j_local // tiny, tiny).transpose(2, 0, 1).reshape(-1)
    order = jnp.asarray(np.eye(side)[source], jnp.bfloat16)
    assert i_out == n_depth
    t = jnp.transpose(amplitudes, (1, 2, 0))
    if gathered:
        t = lax.all_gather(t, "row", axis=1, tiled=True)
        t = t.reshape(n_hi, n_lo, i_out, j_count // n_row, n_row, kc)
        t = jnp.transpose(t, (1, 0, 4, 2, 3, 5)).reshape(rows_all, kc)
        tg = pltpu.VMEM(t.shape, jnp.float32)
    else:
        t = t.reshape(n_depth, i_out, j_local, kc)
        tg = pltpu.VMEM((n_row,) + t.shape, jnp.float32)
    dma = pltpu.SemaphoreType.DMA
    out = pl.pallas_call(
        functools.partial(kernel, sizes, gathered),
        out_shape=jax.ShapeDtypeStruct((rows_r, n_row * n_col * ab_rows), jnp.float32),
        in_specs=[pl.BlockSpec(memory_space=pl.ANY)] * 2 + [pl.BlockSpec(memory_space=pltpu.VMEM)],
        out_specs=pl.BlockSpec(memory_space=pltpu.VMEM),
        scratch_shapes=[
            pltpu.VMEM((n_col, ab_rows, kc), jnp.float32),
            tg,
            tg,
            pltpu.VMEM((2, rows_all, kc), jnp.bfloat16),
            pltpu.VMEM((2, rows_all, kc), jnp.bfloat16),
            pltpu.VMEM((slots, rows_all, CHUNK), jnp.float32),
            pltpu.VMEM((slots, rows_lo, CHUNK), jnp.float32),
            pltpu.VMEM((slots, max(n_hi - 1, 1), rows_d, CHUNK), jnp.float32),
            pltpu.VMEM((slots, rows_d, CHUNK), jnp.float32),
            pltpu.VMEM((late, rows_all // n_g, CHUNK), jnp.float32),
            pltpu.VMEM((late, rows_lo // n_g, CHUNK), jnp.float32),
            pltpu.VMEM((late, max(n_hi - 1, 1), rows_d // n_g, CHUNK), jnp.float32),
            pltpu.VMEM((late, rows_d // n_g, CHUNK), jnp.float32),
            pltpu.VMEM((n_ch, 2, kc, CHUNK), jnp.bfloat16),
            dma((2,)),
            dma((2, n_col, ab_rows // CHUNK)),
            dma((n_col, ab_rows // CHUNK)),
            dma((max(n_row - 1, 1), n_depth)),
            dma((max(n_row - 1, 1), n_depth)),
            dma((slots,)),
            dma((slots,)),
            dma((slots, max(n_hi - 1, 1))),
            dma((slots, max(n_hi - 1, 1))),
            dma((slots, max(n_row - 1, 1))),
            dma((slots, max(n_row - 1, 1))),
            dma((n_depth,)),
            dma((n_depth,)),
            dma((n_depth, max(n_row - 1, 1))),
            dma((n_depth, max(n_row - 1, 1))),
            dma((n_depth, max(n_row - 1, 1))),
            dma((n_depth, max(n_row - 1, 1))),
            dma((late,)),
            dma((late,)),
            dma((late, max(n_hi - 1, 1))),
            dma((late, max(n_hi - 1, 1))),
            dma((late, n_row)),
            dma((late, n_row)),
        ],
        compiler_params=pltpu.CompilerParams(
            collective_id=0, has_side_effects=True, vmem_limit_bytes=60 * 2**20
        ),
        cost_estimate=pl.CostEstimate(
            flops=6 * rows_all * kc * ab_rows * n_col, bytes_accessed=6 * 2**20, transcendentals=0
        ),
    )(integrals, t, order)
    return out.reshape(i_out, j_count // n_row, n_row * n_col * ab_rows)


def solution(mesh):
    sizes = (mesh.shape["row"], mesh.shape["col"], mesh.shape["depth"])
    placed = (P(("row", "col"), "depth"), P("depth", "col", "row"))
    return jax.shard_map(
        functools.partial(shards, sizes),
        mesh=mesh,
        in_specs=placed,
        out_specs=P(("col", "depth"), "row", None),
        check_vma=False,
    )
```

```python
import functools

import jax
import jax.numpy as jnp
import numpy as np
from jax import lax
from jax.experimental import pallas as pl
from jax.experimental.pallas import tpu as pltpu
from jax.sharding import PartitionSpec as P

MESH = pl.DeviceIdType.MESH
CHUNK = 256
LANES = 2


def halves(x):
    hi = x.astype(jnp.bfloat16)
    lo = (x - hi.astype(jnp.float32)).astype(jnp.bfloat16)
    return hi, lo


def kernel(sizes, gathered, w_ref, t_ref, order_ref, out_ref, wg, tg, tg2, th, tl, part, recv1, recv2, fin,
           part_d, recv1_d, recv2_d, fin_d, w_far,
           own_sem, w_send, w_recv, t_send, t_recv, s1_send, s1_recv, s2_send, s2_recv, r_send, r_recv,
           e_send, e_recv, f_send, f_recv, x_send, x_recv, d1_send, d1_recv, d2_send, d2_recv, d_send, d_recv):
    n_row, n_col, n_depth = sizes
    n_lo = LANES
    n_hi = n_depth // n_lo
    ab_rows = w_ref.shape[0]
    n_ch = ab_rows // CHUNK
    assert n_ch == 2 and n_depth == 4 and n_col == 4
    steps = n_col * n_ch
    rows_all = th.shape[1]
    rows_lo = rows_all // n_lo
    rows_d = rows_lo // n_hi
    rows_r = rows_d // n_row
    row, col, depth = lax.axis_index("row"), lax.axis_index("col"), lax.axis_index("depth")
    hi, lo = depth // n_lo, depth % n_lo

    def row_peer(o):
        return (row + o) % n_row

    def hi_peer(o):
        return (hi + o) % n_hi

    mate = hi * n_lo + (1 - lo)
    at_end = (col == 0) | (col == n_col - 1)
    helps = (col == 1) | (col == n_col - 2)
    far = jnp.where(col < n_col // 2, n_col - 1, 0)
    end_col = jnp.where(col < n_col // 2, 0, n_col - 1)
    help_col = jnp.where(col < n_col // 2, 1, n_col - 2)
    normal = jnp.where(at_end, steps - n_ch, steps)

    barrier = pltpu.get_barrier_semaphore()
    for o in range(1, n_row):
        pl.semaphore_signal(barrier, inc=1, device_id={"row": row_peer(o)}, device_id_type=MESH)
    pl.semaphore_signal(barrier, inc=1, device_id={"depth": mate}, device_id_type=MESH)
    for o in range(1, n_hi):
        pl.semaphore_signal(barrier, inc=1, device_id={"depth": hi_peer(o) * n_lo + lo}, device_id_type=MESH)

    @pl.when(col > 0)
    def _():
        pl.semaphore_signal(barrier, inc=1, device_id={"col": col - 1}, device_id_type=MESH)

    @pl.when(col < n_col - 1)
    def _():
        pl.semaphore_signal(barrier, inc=1, device_id={"col": col + 1}, device_id_type=MESH)

    for o in range(1, n_row):

        @pl.when(at_end)
        def _():
            pl.semaphore_signal(
                barrier, inc=1, device_id={"row": row_peer(o), "col": help_col}, device_id_type=MESH
            )

        @pl.when(helps)
        def _():
            pl.semaphore_signal(
                barrier, inc=1, device_id={"row": row_peer(o), "col": end_col}, device_id_type=MESH
            )

    fixed = (n_row - 1) + 1 + (n_hi - 1)
    ends = jnp.where(col > 0, 1, 0) + jnp.where(col < n_col - 1, 1, 0)
    diagonal = jnp.where(at_end | helps, n_row - 1, 0)
    pl.semaphore_wait(barrier, fixed + ends + diagonal)

    def w_copy(src, b, h, side):
        rows = pl.ds(pl.multiple_of(h * CHUNK, CHUNK), CHUNK)
        to = jnp.clip(col + (1 if side else -1), 0, n_col - 1)
        return pltpu.make_async_remote_copy(
            src_ref=w_ref.at[rows] if src is None else wg.at[b, rows],
            dst_ref=wg.at[b, rows],
            send_sem=w_send.at[side, b, h],
            recv_sem=w_recv.at[b, h],
            device_id={"col": to},
            device_id_type=MESH,
        )

    def own_sends(act, h):
        @pl.when(col > 0)
        def _():
            getattr(w_copy(None, col, h, 0), act)()

        @pl.when(col < n_col - 1)
        def _():
            getattr(w_copy(None, col, h, 1), act)()

    def near_sends(act, h):
        @pl.when((col > 0) & goes_right(col - 1))
        def _():
            getattr(w_copy(wg, col - 1, h, 1), act)()

        @pl.when((col < n_col - 1) & goes_left(col + 1))
        def _():
            getattr(w_copy(wg, col + 1, h, 0), act)()

    def near_arrive(h):
        @pl.when(col > 0)
        def _():
            w_copy(wg, col - 1, h, 0).wait_recv()

        @pl.when(col < n_col - 1)
        def _():
            w_copy(wg, col + 1, h, 0).wait_recv()

    def goes_right(b):
        return (col < n_col - 1) & ((b > 0) | (col < n_col - 2))

    def goes_left(b):
        return (col > 0) & ((b < n_col - 1) | (col > 1))

    own_sends("start", 0)

    def t_copy(o):
        return pltpu.make_async_remote_copy(
            src_ref=t_ref,
            dst_ref=tg.at[row],
            send_sem=t_send.at[o - 1],
            recv_sem=t_recv.at[o - 1],
            device_id={"row": row_peer(o)},
            device_id_type=MESH,
        )

    if not gathered:
        for o in range(1, n_row):
            t_copy(o).start()
        t_own = pltpu.make_async_copy(t_ref, tg.at[row], own_sem.at[1])
    else:
        t_own = pltpu.make_async_copy(t_ref, tg, own_sem.at[1])
    t_own.start()
    w_own = pltpu.make_async_copy(w_ref, wg.at[col], own_sem.at[0])
    w_own.start()

    def place(src, q):
        i_out, j_local, kc = t_ref.shape[1:]
        per_r = j_local // n_row
        order = order_ref[...]

        def body(d, c):
            x = src[q, d].reshape(i_out * j_local, kc)
            base = (d % n_lo) * rows_lo + (d // n_lo) * rows_d
            for x_part, into in zip(halves(x), (th, tl)):
                y = jnp.dot(order, x_part, preferred_element_type=jnp.float32).astype(jnp.bfloat16)
                for n in range(n_row * i_out):
                    at = base + n * (per_r * n_row) + q * per_r
                    into[0, pl.ds(pl.multiple_of(at, per_r), per_r), :] = y[n * per_r : (n + 1) * per_r]
            return c

        lax.fori_loop(0, n_depth, body, 0)

    def place_piece(q, p):
        i_out, j_local, kc = t_ref.shape[1:]
        per_r = j_local // n_row
        x = tg2[q, :, p].reshape(n_depth * j_local, kc)
        for x_part, into in zip(halves(x), (th, tl)):
            y = jnp.dot(order_ref[...], x_part, preferred_element_type=jnp.float32).astype(jnp.bfloat16)
            for n in range(n_row * n_depth):
                r, d = n // n_depth, n % n_depth
                base = p * rows_all + (d % n_lo) * rows_lo + (d // n_lo) * rows_d + r * rows_r
                at = base // n_depth + q * per_r
                into[1, pl.ds(pl.multiple_of(at, per_r), per_r), :] = y[n * per_r : (n + 1) * per_r]

    def plain_groups():
        for d in range(n_depth):
            base = (d % n_lo) * rows_lo + (d // n_lo) * rows_d
            x = tg2[pl.ds(base, rows_d), :].reshape(n_row, 2, rows_r // 2, -1)
            for g in range(2):
                at = pl.ds((g * rows_all + base) // 2, rows_d // 2)
                th[1, at, :], tl[1, at, :] = halves(x[:, g].reshape(rows_d // 2, -1))

    def plain():
        def body(m, c):
            at = pl.ds(pl.multiple_of(m * 64, 64), 64)
            th[0, at, :], tl[0, at, :] = halves(tg[at, :])
            return c

        lax.fori_loop(0, rows_all // 64, body, 0)

    piece = rows_all // n_depth
    n_swap = n_depth - 1
    n_g = 2 if gathered else n_depth

    def e_copy(p):
        rows = pl.ds(p * piece, piece)
        return pltpu.make_async_remote_copy(
            src_ref=t_ref.at[rows] if gathered else t_ref.at[:, p],
            dst_ref=tg2.at[rows] if gathered else tg2.at[row, :, p],
            send_sem=e_send.at[p],
            recv_sem=e_recv.at[p],
            device_id={"col": help_col},
            device_id_type=MESH,
        )

    def x_copy(p, o):
        return pltpu.make_async_remote_copy(
            src_ref=tg2.at[row, :, p],
            dst_ref=tg2.at[row, :, p],
            send_sem=x_send.at[p, o - 1],
            recv_sem=x_recv.at[p, o - 1],
            device_id={"row": row_peer(o)},
            device_id_type=MESH,
        )

    def f_copy(p, o):
        q = (row + n_row - o) % n_row
        return pltpu.make_async_remote_copy(
            src_ref=tg.at[q, :, p],
            dst_ref=tg2.at[q, :, p],
            send_sem=f_send.at[p, o - 1],
            recv_sem=f_recv.at[p, o - 1],
            device_id={"col": help_col},
            device_id_type=MESH,
        )

    def take(p):
        e_copy(p).wait_recv()
        if not gathered and p < n_swap:
            for o in range(1, n_row):
                x_copy(p, o).start()

    def place_own(p):
        if not gathered:
            place_piece(row, p)

    def place_peers(p):
        if not gathered:
            for o in range(1, n_row):
                (x_copy if p < n_swap else f_copy)(p, o).wait_recv()
                place_piece((row + n_row - o) % n_row, p)

    t_own.wait()
    if not gathered:
        place(tg, row)
    else:
        plain()

    own_sends("wait_send", 0)
    own_sends("start", 1)
    near_arrive(0)
    own_sends("wait_send", 1)
    near_sends("start", 0)

    @pl.when(at_end)
    def _():
        for p in range(n_swap):
            e_copy(p).start()

    near_arrive(1)
    if not gathered:
        for o in range(1, n_row):
            t_copy(o).wait_recv()
            place(tg, (row + n_row - o) % n_row)
    w_own.wait()

    near = jnp.minimum(col, n_col - 1 - col)

    def block_at(k):
        p, h = k // n_ch, k % n_ch
        both = p <= 2 * near
        s = jnp.where(both, (p + 1) // 2, p - near)
        left = jnp.where(both, p % 2 == 1, col > near)
        b = jnp.where(p == 0, col, jnp.where(left, col - s, col + s))
        return b, h, s

    def s1_copy(k):
        return pltpu.make_async_remote_copy(
            src_ref=part.at[k, pl.ds(pl.multiple_of((1 - lo) * rows_lo, rows_lo), rows_lo)],
            dst_ref=recv1.at[k],
            send_sem=s1_send.at[k],
            recv_sem=s1_recv.at[k],
            device_id={"depth": mate},
            device_id_type=MESH,
        )

    def s2_copy(k, o):
        return pltpu.make_async_remote_copy(
            src_ref=part.at[k, pl.ds(pl.multiple_of(lo * rows_lo + hi_peer(o) * rows_d, rows_d), rows_d)],
            dst_ref=recv2.at[k, o - 1],
            send_sem=s2_send.at[k, o - 1],
            recv_sem=s2_recv.at[k, o - 1],
            device_id={"depth": hi_peer(o) * n_lo + lo},
            device_id_type=MESH,
        )

    def out_cols(b, h):
        return pl.ds(pl.multiple_of((row * n_col + b) * ab_rows + h * CHUNK, CHUNK), CHUNK)

    def r_copy(k, o):
        return pltpu.make_async_remote_copy(
            src_ref=fin.at[k, pl.ds(pl.multiple_of(row_peer(o) * rows_r, rows_r), rows_r)],
            dst_ref=out_ref.at[:, out_cols(*block_at(k)[:2])],
            send_sem=r_send.at[k, o - 1],
            recv_sem=r_recv.at[k, o - 1],
            device_id={"row": row_peer(o)},
            device_id_type=MESH,
        )

    def d1_copy(n):
        return pltpu.make_async_remote_copy(
            src_ref=part_d.at[n, pl.ds(pl.multiple_of((1 - lo) * (rows_lo // n_g), rows_lo // n_g), rows_lo // n_g)],
            dst_ref=recv1_d.at[n],
            send_sem=d1_send.at[n],
            recv_sem=d1_recv.at[n],
            device_id={"depth": mate},
            device_id_type=MESH,
        )

    def d2_copy(n, o):
        start = lo * (rows_lo // n_g) + hi_peer(o) * (rows_d // n_g)
        return pltpu.make_async_remote_copy(
            src_ref=part_d.at[n, pl.ds(pl.multiple_of(start, rows_d // n_g), rows_d // n_g)],
            dst_ref=recv2_d.at[n, o - 1],
            send_sem=d2_send.at[n, o - 1],
            recv_sem=d2_recv.at[n, o - 1],
            device_id={"depth": hi_peer(o) * n_lo + lo},
            device_id_type=MESH,
        )

    def d_copy(n, o):
        g, h = n // n_ch, n % n_ch
        half = rows_r // n_g
        return pltpu.make_async_remote_copy(
            src_ref=fin_d.at[n, pl.ds(pl.multiple_of(row_peer(o) * half, half), half)],
            dst_ref=out_ref.at[pl.ds(g * half, half), out_cols(far, h)],
            send_sem=d_send.at[n, o],
            recv_sem=d_recv.at[n, o],
            device_id={"row": row_peer(o), "col": end_col},
            device_id_type=MESH,
        )

    def multiply(w_halves, which, first, tile):
        wh, wl = w_halves
        w3 = jnp.concatenate([wh, wh, wl], axis=0)
        for start in first:
            at = pl.ds(start, tile)
            a = th[which, at, :]
            a3 = jnp.concatenate([a, tl[which, at, :], a], axis=1)
            yield start, jnp.dot(a3, w3, preferred_element_type=jnp.float32)

    def d_multiply(n):
        rows = rows_all // n_g
        h = n % n_ch
        for _, y in multiply((w_far[h, 0], w_far[h, 1]), 1, (n // n_ch * rows,), rows):
            part_d[n] = y
        d1_copy(n).start()

    def d_pair(n):
        d1_copy(n).wait_recv()
        at = pl.ds(pl.multiple_of(lo * (rows_lo // n_g), rows_lo // n_g), rows_lo // n_g)
        part_d[n, at, :] = part_d[n, at, :] + recv1_d[n]
        for o in range(1, n_hi):
            d2_copy(n, o).start()

    def d_finish(n):
        start = lo * (rows_lo // n_g) + hi * (rows_d // n_g)
        total = part_d[n, pl.ds(pl.multiple_of(start, rows_d // n_g), rows_d // n_g), :]
        for o in range(1, n_hi):
            d2_copy(n, o).wait_recv()
            total = total + recv2_d[n, o - 1]
        fin_d[n] = total
        for o in range(n_row):
            d_copy(n, o).start()

    def pair(j):
        s1_copy(j).wait_recv()
        at = pl.ds(pl.multiple_of(lo * rows_lo, rows_lo), rows_lo)
        part[j, at, :] = part[j, at, :] + recv1[j]
        for o in range(1, n_hi):
            s2_copy(j, o).start()

    def finish(j):
        total = part[j, pl.ds(pl.multiple_of(lo * rows_lo + hi * rows_d, rows_d), rows_d), :]
        for o in range(1, n_hi):
            s2_copy(j, o).wait_recv()
            total = total + recv2[j, o - 1]
        fin[j] = total
        for o in range(1, n_row):
            r_copy(j, o).start()
        mine = fin[j, pl.ds(pl.multiple_of(row * rows_r, rows_r), rows_r), :]
        out_ref[:, out_cols(*block_at(j)[:2])] = mine

    def step(k, c):
        @pl.when(helps & (k == 1))
        def _():
            take(0)

        @pl.when(helps & (k == 3))
        def _():
            take(1)

        @pl.when(helps & (k == 4))
        def _():
            take(2)

        @pl.when(helps & (k == steps - 1))
        def _():
            place_own(0)
            place_own(1)
            place_peers(0)

        @pl.when(k == 3)
        def _():
            near_sends("wait_send", 0)
            near_sends("start", 1)

        for p in range(n_swap, n_depth):

            @pl.when(at_end & (k == 2 * (p - n_swap)))
            def _():
                e_copy(p - n_swap).wait_send()
                e_copy(p).start()
                if not gathered:
                    for o in range(1, n_row):
                        f_copy(p, o).start()

        b, h, s = block_at(k)

        @pl.when(s >= 2)
        def _():
            w_copy(wg, b, h, 0).wait_recv()

        w_halves = halves(wg[b, pl.ds(pl.multiple_of(h * CHUNK, CHUNK), CHUNK), :].T)

        @pl.when(helps & (k >= steps - n_ch))
        def _():
            w_far[h, 0], w_far[h, 1] = w_halves

        for start, y in multiply(w_halves, 0, (0, rows_all // 2), rows_all // 2):
            part[k, pl.ds(start, rows_all // 2), :] = y
        s1_copy(k).start()

        @pl.when(k >= 1)
        def _():
            pair(k - 1)

        @pl.when(k >= 2)
        def _():
            finish(k - 2)

        return c

    lax.fori_loop(0, normal, step, 0)

    def group(act, g):
        for h in range(n_ch):
            act(g * n_ch + h)

    @pl.when(helps)
    def _():
        place_peers(1)
        if gathered:
            for p in range(n_swap, n_depth):
                take(p)
            plain_groups()
        group(d_multiply, 0)

    pair(normal - 1)
    finish(normal - 2)

    @pl.when(helps)
    def _():
        group(d_multiply, 1)
        group(d_pair, 0)

    finish(normal - 1)

    @pl.when(helps)
    def _():
        group(d_pair, 1)
        group(d_finish, 0)
        group(d_finish, 1)
        for g in range(2, n_g):
            if g >= n_swap:
                take(g)
            place_own(g)
            place_peers(g)
            group(d_multiply, g)
            if g > 2:
                group(d_finish, g - 1)
            group(d_pair, g)
        if n_g > 2:
            group(d_finish, n_g - 1)

    def drain(k, c):
        s1_copy(k).wait_send()
        for o in range(1, n_hi):
            s2_copy(k, o).wait_send()
        for o in range(1, n_row):
            r_copy(k, o).wait_send()
            r_copy(k, o).wait_recv()
        return c

    lax.fori_loop(0, normal, drain, 0)

    @pl.when(helps)
    def _():
        for n in range(n_g * n_ch):
            d1_copy(n).wait_send()
            for o in range(1, n_hi):
                d2_copy(n, o).wait_send()
            for o in range(n_row):
                d_copy(n, o).wait_send()

    near_sends("wait_send", 1)

    @pl.when(at_end)
    def _():
        for p in range(n_depth - n_swap, n_swap):
            e_copy(p).wait_send()
        for p in range(n_swap, n_depth):
            e_copy(p).wait_send()
            if not gathered:
                for o in range(1, n_row):
                    f_copy(p, o).wait_send()
        for n in range(n_g * n_ch):
            for o in range(n_row):
                d_copy(n, o).wait_recv()

    if not gathered:

        @pl.when(helps)
        def _():
            for p in range(n_swap):
                for o in range(1, n_row):
                    x_copy(p, o).wait_send()

    if not gathered:
        for o in range(1, n_row):
            t_copy(o).wait_send()


def shards(sizes, integrals, amplitudes):
    n_row, n_col, n_depth = sizes
    n_lo = LANES
    n_hi = n_depth // n_lo
    kc, i_count, j_local = amplitudes.shape
    j_count = j_local * n_row
    ab_rows = integrals.shape[0]
    n_ch = ab_rows // CHUNK
    slots = n_col * n_ch
    n_g = 2 if j_local % (16 * n_row) != 0 else n_depth
    late = n_g * n_ch
    rows_all = i_count * j_count
    rows_lo = rows_all // n_lo
    rows_d = rows_lo // n_hi
    rows_r = rows_d // n_row
    i_out = i_count // n_depth
    gathered = j_local % (16 * n_row) != 0
    side = i_out * j_local
    tiny = j_local if gathered else n_row
    source = np.arange(side).reshape(i_out, j_local // tiny, tiny).transpose(2, 0, 1).reshape(-1)
    order = jnp.asarray(np.eye(side)[source], jnp.bfloat16)
    assert i_out == n_depth
    t = jnp.transpose(amplitudes, (1, 2, 0))
    if gathered:
        t = lax.all_gather(t, "row", axis=1, tiled=True)
        t = t.reshape(n_hi, n_lo, i_out, j_count // n_row, n_row, kc)
        t = jnp.transpose(t, (1, 0, 4, 2, 3, 5)).reshape(rows_all, kc)
        tg = pltpu.VMEM(t.shape, jnp.float32)
    else:
        t = t.reshape(n_depth, i_out, j_local, kc)
        tg = pltpu.VMEM((n_row,) + t.shape, jnp.float32)
    dma = pltpu.SemaphoreType.DMA
    out = pl.pallas_call(
        functools.partial(kernel, sizes, gathered),
        out_shape=jax.ShapeDtypeStruct((rows_r, n_row * n_col * ab_rows), jnp.float32),
        in_specs=[pl.BlockSpec(memory_space=pl.ANY)] * 2 + [pl.BlockSpec(memory_space=pltpu.VMEM)],
        out_specs=pl.BlockSpec(memory_space=pltpu.VMEM),
        scratch_shapes=[
            pltpu.VMEM((n_col, ab_rows, kc), jnp.float32),
            tg,
            tg,
            pltpu.VMEM((2, rows_all, kc), jnp.bfloat16),
            pltpu.VMEM((2, rows_all, kc), jnp.bfloat16),
            pltpu.VMEM((slots, rows_all, CHUNK), jnp.float32),
            pltpu.VMEM((slots, rows_lo, CHUNK), jnp.float32),
            pltpu.VMEM((slots, max(n_hi - 1, 1), rows_d, CHUNK), jnp.float32),
            pltpu.VMEM((slots, rows_d, CHUNK), jnp.float32),
            pltpu.VMEM((late, rows_all // n_g, CHUNK), jnp.float32),
            pltpu.VMEM((late, rows_lo // n_g, CHUNK), jnp.float32),
            pltpu.VMEM((late, max(n_hi - 1, 1), rows_d // n_g, CHUNK), jnp.float32),
            pltpu.VMEM((late, rows_d // n_g, CHUNK), jnp.float32),
            pltpu.VMEM((n_ch, 2, kc, CHUNK), jnp.bfloat16),
            dma((2,)),
            dma((2, n_col, ab_rows // CHUNK)),
            dma((n_col, ab_rows // CHUNK)),
            dma((max(n_row - 1, 1),)),
            dma((max(n_row - 1, 1),)),
            dma((slots,)),
            dma((slots,)),
            dma((slots, max(n_hi - 1, 1))),
            dma((slots, max(n_hi - 1, 1))),
            dma((slots, max(n_row - 1, 1))),
            dma((slots, max(n_row - 1, 1))),
            dma((n_depth,)),
            dma((n_depth,)),
            dma((n_depth, max(n_row - 1, 1))),
            dma((n_depth, max(n_row - 1, 1))),
            dma((n_depth, max(n_row - 1, 1))),
            dma((n_depth, max(n_row - 1, 1))),
            dma((late,)),
            dma((late,)),
            dma((late, max(n_hi - 1, 1))),
            dma((late, max(n_hi - 1, 1))),
            dma((late, n_row)),
            dma((late, n_row)),
        ],
        compiler_params=pltpu.CompilerParams(
            collective_id=0, has_side_effects=True, vmem_limit_bytes=60 * 2**20
        ),
        cost_estimate=pl.CostEstimate(
            flops=6 * rows_all * kc * ab_rows * n_col, bytes_accessed=6 * 2**20, transcendentals=0
        ),
    )(integrals, t, order)
    return out.reshape(i_out, j_count // n_row, n_row * n_col * ab_rows)


def solution(mesh):
    sizes = (mesh.shape["row"], mesh.shape["col"], mesh.shape["depth"])
    placed = (P(("row", "col"), "depth"), P("depth", "col", "row"))
    return jax.shard_map(
        functools.partial(shards, sizes),
        mesh=mesh,
        in_specs=placed,
        out_specs=P(("col", "depth"), "row", None),
        check_vma=False,
    )
```
